512 devices in a mesh: sec: 8 (over x, core), row: 8 (over y, z_hi), col: 8 (over z_lo).
Axes of the slice: x: 4, y: 4, z: 16 (z_hi: 2, z_lo: 8; z = z_hi * 8 + z_lo), core: 2. Of those that a mesh axis runs over, the one named last changes fastest.
Arguments:
- images: float32 [16, 3072, 3072], P('sec', 'row', 'col'), may hold values from -18 to 18
- offsets: int32 [2, 16, 24, 24], P(None, 'sec', 'row', 'col'), may hold values from -64 to 64
- warp: float32 [2, 16, 24, 24], P(None, 'sec', 'row', 'col'), may hold values from -2 to 2
- stiffness: float32 [2, 16, 24, 24], P(None, 'sec', 'row', 'col'), may hold values from 0.04 to 0.25
- valid: int32 [16, 24, 24], P('sec', 'row', 'col'), may hold values 0 or 1
Outputs:
- displacement: float32 [2, 16, 24, 24], P(None, 'sec', 'row', 'col')
- warped: float32 [2, 16, 24, 24], P(None, 'sec', 'row', 'col')
The draws below stay inside these ranges and needn't reach their ends.
All inputs are finite; a program needn't handle non-finite values. No bound on the sum of `valid` on one device may be relied on, other than what follows from the above.
Results may differ from the reference program's by a relative error of at most 0.0003.
Values sent between devices are 32-bit elements; how exact they have to be, the bound alone decides.
A program may use at most 64 MiB of HBM per device.

```python
import math
import jax
import jax.numpy as jnp
from jax import lax

P_SIZE = 128
MAXOFF = 64
ITERS = 3
NSEC = 16
PR = 24
PC = 24
H = 3072
W = 3072


def draw_images(key, part):
    key = jax.random.fold_in(key, 7)
    base_key, noise_key = jax.random.split(key, 2)
    common = jax.random.truncated_normal(base_key, -6.0, 6.0, (H, W), jnp.float32)
    noise = jax.random.truncated_normal(noise_key, -6.0, 6.0, (NSEC, H, W), jnp.float32)
    return 0.2 * common + 0.98 * noise


def plant(entries, key, smallest, largest):
    place = [jax.random.randint(jax.random.fold_in(key, axis), (), 0, length) for axis, length in enumerate(entries.shape)]
    main_axis = entries.shape.index(max(entries.shape))
    beside = place[:main_axis] + [(place[main_axis] + 1) % entries.shape[main_axis]] + place[main_axis + 1:]
    return entries.at[tuple(place)].set(smallest).at[tuple(beside)].set(largest)


def shard_levels(own_key, extent, pieces, low, top_value):
    factor_of = 1.0
    for axis_at, blocks in pieces:
        heights = jax.random.uniform(jax.random.fold_in(jax.random.fold_in(own_key, 6), axis_at), (blocks,), jnp.float32, low / len(pieces), top_value / len(pieces))
        factor_of = factor_of * jnp.repeat(jnp.exp(heights), extent[axis_at] // blocks).reshape((-1,) + (1,) * (len(extent) - 1 - axis_at))
    return factor_of


def gaussian(rng, extent, spread, most, cuts=(), kind=jnp.bfloat16):
    array = spread * jax.random.normal(rng, extent, jnp.float32)
    if cuts:
        array = array * shard_levels(rng, extent, cuts, -0.22, 0.18)
    return jnp.clip(array, -most, most).astype(kind)


def setup_inputs(seed: int = 0) -> dict:
    key_of = jax.random.split(jax.random.key(seed), 6)
    images = draw_images(jax.random.fold_in(key_of[5], 71), 0)
    offsets = plant(jax.random.randint(key_of[1], (2, NSEC, PR, PC), -MAXOFF, MAXOFF + 1), jax.random.fold_in(key_of[1], 1), -MAXOFF, MAXOFF).astype(jnp.int32)
    warp = gaussian(key_of[2], (2, NSEC, PR, PC), 0.3, 2.0, ((1, 8), (2, 8), (3, 8)), jnp.float32)
    stiffness = jnp.clip(jnp.exp(math.log(0.25) - 1.8325815 * jax.random.uniform(key_of[3], (2, NSEC, PR, PC), jnp.float32) ** shard_levels(key_of[3], (2, NSEC, PR, PC), ((1, 8), (2, 8), (3, 8)), -0.2, 0.2)), 0.04, 0.25)
    valid = plant((jax.random.randint(key_of[4], (NSEC, PR, PC), 0, 4) < 3).astype(jnp.int32), jax.random.fold_in(key_of[4], 1), 0, 1)
    return {"images": images, "offsets": offsets, "warp": warp, "stiffness": stiffness, "valid": valid}


SHARPNESS = 80.0
ANCHOR_STIFFNESS = 0.2


def expectation(scores):
    half_side = P_SIZE // 2
    coords = ((jnp.arange(P_SIZE, dtype=jnp.int32) + half_side) % P_SIZE - half_side).astype(jnp.float32)
    highest = jnp.max(scores, axis=(1, 2), keepdims=True)
    weights = jnp.exp(scores - highest)
    total = jnp.sum(weights, axis=(1, 2))
    along_rows = jnp.sum(weights * coords[None, :, None], axis=(1, 2)) / total
    along_cols = jnp.sum(weights * coords[None, None, :], axis=(1, 2)) / total
    return along_rows, along_cols


def soft_peak(mine, theirs):
    mine = mine - jnp.mean(mine, axis=(1, 2), keepdims=True)
    theirs = theirs - jnp.mean(theirs, axis=(1, 2), keepdims=True)
    product = jnp.conj(jnp.fft.fft2(mine)) * jnp.fft.fft2(theirs)
    correlation = jnp.real(jnp.fft.ifft2(product)).astype(jnp.float32)
    scores = correlation * (SHARPNESS / (P_SIZE * P_SIZE))
    return expectation(scores)


def pull(current, right_nb, left_nb, down_nb, upper_nb, right, right_left, down, down_upper, anchor, target):
    return (current + right * (right_nb - current) + right_left * (left_nb - current)
            + down * (down_nb - current) + down_upper * (upper_nb - current) + anchor * (target - current))


def reference(images, offsets, warp, stiffness, valid):
    row_start = jnp.arange(PR, dtype=jnp.int32) * P_SIZE
    col_start = jnp.arange(PC, dtype=jnp.int32) * P_SIZE
    following = jnp.concatenate([images[1:], jnp.zeros_like(images[:1])], 0)

    def per_section(packed):
        current, upcoming, shift_pair = packed
        own = current.reshape(PR, P_SIZE, PC, P_SIZE).transpose(0, 2, 1, 3)
        padded = jnp.pad(upcoming, MAXOFF)
        starts_row = (MAXOFF + row_start[:, None] + shift_pair[0]).astype(jnp.int32)
        starts_col = (MAXOFF + col_start[None, :] + shift_pair[1]).astype(jnp.int32)

        def one_row(item):
            own_row, rows_at, cols_at = item
            blocks = jax.vmap(lambda start_row, start_col: lax.dynamic_slice(padded, (start_row, start_col), (P_SIZE, P_SIZE)))(rows_at, cols_at)
            return soft_peak(own_row, blocks)

        along_rows, along_cols = lax.map(one_row, (own, starts_row, starts_col))
        return jnp.stack([along_rows, along_cols])

    peaks = lax.map(per_section, (images, following, jnp.moveaxis(offsets, 1, 0)))
    peaks = jnp.moveaxis(peaks, 0, 1)
    displacement = (offsets.astype(jnp.float32) + peaks) / P_SIZE
    live = jnp.arange(NSEC) < NSEC - 1
    displacement = jnp.where(live[None, :, None, None], displacement, jnp.zeros_like(displacement))
    before = jnp.cumsum(displacement, axis=1) - displacement
    target = warp - before
    right = stiffness[0].at[:, :, -1].set(0.0)
    down = stiffness[1].at[:, -1, :].set(0.0)
    right_left = jnp.pad(right, ((0, 0), (0, 0), (1, 0)))[:, :, :-1]
    down_upper = jnp.pad(down, ((0, 0), (1, 0), (0, 0)))[:, :-1, :]
    anchor = ANCHOR_STIFFNESS * valid.astype(jnp.float32)
    warped = warp
    for iteration in range(ITERS):
        padded = jnp.pad(warped, ((0, 0), (0, 0), (1, 1), (1, 1)))
        warped = pull(warped, padded[:, :, 1:-1, 2:], padded[:, :, 1:-1, :-2], padded[:, :, 2:, 1:-1],
                      padded[:, :, :-2, 1:-1], right, right_left, down, down_upper, anchor, target)
    return displacement, warped
```

```python
import functools

import jax
import jax.numpy as jnp
import ml_dtypes
import numpy as np
from jax import lax
from jax.experimental import pallas as pl
from jax.experimental.pallas import tpu as pltpu
from jax.sharding import PartitionSpec as P

MESH = pl.DeviceIdType.MESH
N = 128
HALF = 64
SIDE = 3
TILE = SIDE * N
BLOCKS = 2 * TILE // N
SHARPNESS = 80.0
ANCHOR = 0.2
ITERS = 3
BF = jnp.bfloat16
F32 = jnp.float32


def split3(a):
    high = a.astype(ml_dtypes.bfloat16)
    rest = a - high.astype(np.float64)
    mid = rest.astype(ml_dtypes.bfloat16)
    low = (rest - mid.astype(np.float64)).astype(ml_dtypes.bfloat16)
    return high, mid, low


def tables():
    x = np.arange(N)
    forward = np.zeros((N, N))
    for f in range(HALF):
        forward[f] = np.cos(2 * np.pi * ((f * x) % N) / N)
    forward[HALF] = 1 - 2 * (x % 2)
    for f in range(1, HALF):
        forward[HALF + f] = np.sin(2 * np.pi * ((f * x) % N) / N)
    scale = np.full(N, 2.0 / N)
    scale[0] = scale[HALF] = 1.0 / N
    inverse = (forward * scale[:, None]).T

    def right(a):
        h, m, l = split3(a)
        return np.block([[h, m], [h, m]]), np.concatenate([h, l], 0)

    def left(a):
        h, m, l = split3(a)
        return np.concatenate([h, m], 1), np.concatenate([h, l], 1)

    return (
        *right(forward.T),
        *left(forward),
        *right(inverse.T),
        *left(inverse * (SHARPNESS / (N * N))),
    )


def parts(x):
    high = x.astype(BF)
    rest = x - high.astype(F32)
    mid = rest.astype(BF)
    low = (rest - mid.astype(F32)).astype(BF)
    return high, mid, low


def dot(a, b):
    return jnp.dot(a, b, preferred_element_type=F32)


def right_mul(x, wa, wb):
    high, mid, low = parts(x)
    a = dot(jnp.concatenate([high, mid], 1), wa)
    return a[:, :N] + a[:, N:] + dot(jnp.concatenate([low, high], 1), wb)


def left_mul(wa, wb, x):
    high, mid, low = parts(x)
    row = jnp.concatenate([high, mid], 1)
    a = dot(wa, jnp.concatenate([row, row], 0))
    return a[:, :N] + a[:, N:] + dot(wb, jnp.concatenate([low, high], 0))


def forward(x, t):
    x = x - jnp.sum(x, keepdims=True) * (1.0 / (N * N))
    return left_mul(t[2][...], t[3][...], right_mul(x, t[0][...], t[1][...]))


def inverse(x, t):
    return left_mul(t[6][...], t[7][...], right_mul(x, t[4][...], t[5][...]))


def iota(shape, dim):
    return lax.broadcasted_iota(jnp.int32, shape, dim)


def swap(x):
    return pltpu.roll(x, HALF, 1)


def cross(mine, theirs):
    lane = iota((N, N), 1)
    single = (lane & (HALF - 1)) == 0
    turned = swap(theirs)
    first = jnp.where(single | (lane < HALF), theirs, -turned)
    second = jnp.where(single, 0.0, jnp.where(lane < HALF, turned, theirs))
    other = swap(mine)
    even, odd = slice(0, HALF), slice(HALF, N)

    def pair(a, b):
        return mine[a] * first[b] + other[a] * second[b]

    lone = iota((HALF, N), 0) == 0
    both = pair(odd, odd)
    top = pair(even, even) + jnp.where(lone, 0.0, both)
    low = jnp.where(lone, both, pair(even, odd) - pair(odd, even))
    return jnp.concatenate([top, low], 0)


def peak(scores, dy, dx):
    rows = (((iota((N, N), 0) - dy + HALF) & (N - 1)) - HALF).astype(F32)
    cols = (((iota((1, N), 1) - dx + HALF) & (N - 1)) - HALF).astype(F32)
    weights = jnp.exp(scores - jnp.max(scores, keepdims=True))
    by_col = jnp.sum(weights, axis=0, keepdims=True)
    total = jnp.sum(by_col, keepdims=True)
    along_rows = jnp.sum(jnp.sum(weights * rows, axis=0, keepdims=True), keepdims=True)
    along_cols = jnp.sum(by_col * cols, keepdims=True)
    return along_rows / total, along_cols / total


def kernel(sizes, images, off, warp, stiff, valid, *rest):
    t = rest[:8]
    disp_ref, warped_ref = rest[8:10]
    (own, ext, spec, packed, landed, small, ptile, pslots, ttile, tslots, dtile, dslots, strips) = rest[10:23]
    lsem, ts, tr, rs, rr, cs, cr, ks, kr, ps, pr, ds, dr, ns, nr = rest[23:]
    ns_, nr_, nc_ = sizes
    s, r, c = lax.axis_index("sec"), lax.axis_index("row"), lax.axis_index("col")

    def inside(a, b, e):
        ok = None
        for at, by, n in ((s, a, ns_), (r, b, nr_), (c, e, nc_)):
            if by:
                here = (at + by >= 0) & (at + by < n)
                ok = here if ok is None else ok & here
        return ok

    def there(a, b, e):
        return (s + a, r + b, c + e)

    locals_ = [
        pltpu.make_async_copy(images.at[0], own, lsem.at[0]),
        pltpu.make_async_copy(images.at[1], ext.at[0, HALF : HALF + TILE, N : N + TILE], lsem.at[1]),
    ]
    for copy in locals_:
        copy.start()

    near = [(a, b) for a in (-1, 0, 1) for b in (-1, 0, 1) if (a, b) != (0, 0)]
    sides = [(-1, 0), (1, 0), (0, -1), (0, 1)]
    goes = [(k, 0, 0) for k in range(1, ns_)] + [(-1, 0, 0)] + [(-1, b, e) for b, e in sides] + [(0, b, e) for b, e in near]
    barrier = pltpu.get_barrier_semaphore()
    expected = 0
    for a, b, e in goes:
        @pl.when(inside(-a, -b, -e))
        def _(a=a, b=b, e=e):
            pl.semaphore_signal(barrier, inc=1, device_id=there(-a, -b, -e), device_id_type=MESH)

        expected = expected + inside(a, b, e).astype(jnp.int32)

    @pl.when(r == 0)
    def _():
        for p in range(2):
            ext[p, 0:HALF, :] = jnp.zeros((HALF, TILE + 2 * N), F32)

    @pl.when(r == nr_ - 1)
    def _():
        for p in range(2):
            ext[p, HALF + TILE :, :] = jnp.zeros((HALF, TILE + 2 * N), F32)

    @pl.when(c == 0)
    def _():
        for p in range(2):
            ext[p, 0:HALF, 0:N] = jnp.zeros((HALF, N), F32)
            ext[p, HALF + TILE :, 0:N] = jnp.zeros((HALF, N), F32)
            landed[p, 0] = jnp.zeros((TILE // 2, N), F32)

    @pl.when(c == nc_ - 1)
    def _():
        for p in range(2):
            ext[p, 0:HALF, N + TILE :] = jnp.zeros((HALF, N), F32)
            ext[p, HALF + TILE :, N + TILE :] = jnp.zeros((HALF, N), F32)
            landed[p, 1] = jnp.zeros((TILE // 2, N), F32)

    @pl.when(s == ns_ - 1)
    def _():
        ext[1] = jnp.zeros((TILE + 2 * HALF, TILE + 2 * N), F32)
        landed[1] = jnp.zeros((2, TILE // 2, N), F32)

    blank = jnp.zeros((8, N), F32)
    for b, e in near:
        @pl.when(jnp.logical_not(inside(0, b, e)))
        def _(b=b, e=e):
            pslots[3 * (b + 1) + e + 1] = blank
            tslots[3 * (b + 1) + e + 1] = blank

    for k in range(ns_):
        @pl.when(s <= k)
        def _(k=k):
            dslots[k] = blank

    row8, lane8 = iota((8, N), 0), iota((8, N), 1)
    small[...] = jnp.zeros_like(small)
    for comp in range(2):
        for sec in range(2):
            small[2 * comp + sec, 0:SIDE, 0:SIDE] = warp[comp, sec]
            small[4 + 2 * comp + sec, 0:SIDE, 0:SIDE] = stiff[comp, sec]
    for sec in range(2):
        small[8 + sec, 0:SIDE, 0:SIDE] = ANCHOR * valid[sec].astype(F32)
    start = jnp.zeros((8, N), F32)
    held = jnp.zeros((8, N), F32)
    for g in range(4):
        sec = g % 2
        w = small[g]
        right = jnp.where((c == nc_ - 1) & (lane8 == SIDE - 1), 0.0, small[4 + sec])
        down = jnp.where((r == nr_ - 1) & (row8 == SIDE - 1), 0.0, small[6 + sec])
        start = start + (pltpu.roll(w, 16 * g, 1) if g else w)
        for q, quantity in enumerate((w, right, down, small[8 + sec])):
            by = 16 * g + SIDE * q
            held = held + (pltpu.roll(quantity, by, 1) if by else quantity)
    ptile[...] = held

    for copy in locals_:
        copy.wait()

    low_lane = iota((TILE // 2, N), 1) < HALF
    for im in range(2):
        for side in range(2):
            if im == 0:
                strip = own[:, 0:N] if side == 0 else own[:, TILE - N :]
            else:
                strip = ext[0, HALF : HALF + TILE, N : 2 * N] if side == 0 else ext[0, HALF : HALF + TILE, TILE : TILE + N]
            upper, lower = strip[: TILE // 2], strip[TILE // 2 :]
            packed[im, side] = jnp.where(low_lane, upper, swap(lower)) if side == 0 else jnp.where(low_lane, swap(upper), lower)

    def mine_spectra(p):
        def step(k, _):
            i, j = k // SIDE, k % SIDE
            at = pl.multiple_of(i * N, N)
            if p == 0:
                block = own[pl.ds(at, N), pl.ds(pl.multiple_of(j * N, N), N)]
            else:
                block = ext[0, pl.ds(pl.multiple_of(at + HALF, HALF), N), pl.ds(pl.multiple_of(j * N + N, N), N)]
            spec[9 * p + k] = forward(block, t)
            return 0

        lax.fori_loop(0, SIDE * SIDE, step, 0)

    mine_spectra(0)

    pl.semaphore_wait(barrier, expected)

    def remote(src, dst, send, recv, target):
        return pltpu.make_async_remote_copy(
            src_ref=src, dst_ref=dst, send_sem=send, recv_sem=recv, device_id=target, device_id_type=MESH
        )

    def col_rim(p, side):
        e = 2 * side - 1
        return remote(
            packed.at[1 - p, side], landed.at[p, 1 - side], cs.at[2 * p + side], cr.at[2 * p + 1 - side], there(-p, 0, e)
        )

    def row_rim(p, side):
        b = 2 * side - 1
        src = images.at[1 - p, TILE - HALF : TILE, :] if side else images.at[1 - p, 0:HALF, :]
        at = slice(0, HALF) if side else slice(HALF + TILE, 2 * HALF + TILE)
        return remote(src, ext.at[p, at, N : N + TILE], rs.at[2 * p + side], rr.at[2 * p + 1 - side], there(-p, b, 0))

    def corner(p, end, side):
        e = 2 * side - 1
        at = slice(HALF + TILE, 2 * HALF + TILE) if end else slice(0, HALF)
        src = slice(TILE, TILE + N) if side else slice(N, 2 * N)
        dst = slice(0, N) if side else slice(N + TILE, 2 * N + TILE)
        n = 4 * p + 2 * end
        return remote(ext.at[p, at, src], ext.at[p, at, dst], ks.at[n + side], kr.at[n + 1 - side], there(0, 0, e))

    def tile_copy():
        return remote(images.at[0], ext.at[1, HALF : HALF + TILE, N : N + TILE], ts.at[0], tr.at[0], there(-1, 0, 0))

    def frame_copy(src, slots, send, recv, b, e):
        n, m = 3 * (b + 1) + e + 1, 3 * (1 - b) + 1 - e
        return remote(src, slots.at[m], send.at[n], recv.at[m], there(0, b, e))

    for b, e in near:
        @pl.when(inside(0, b, e))
        def _(b=b, e=e):
            frame_copy(ptile, pslots, ps, pr, b, e).start()

    for p in (0, 1):
        for side in range(2):
            @pl.when(inside(-p, 0, 2 * side - 1))
            def _(p=p, side=side):
                col_rim(p, side).start()
    for p in (1, 0):
        for side in range(2):
            @pl.when(inside(-p, 2 * side - 1, 0))
            def _(p=p, side=side):
                row_rim(p, side).start()

    @pl.when(s > 0)
    def _():
        tile_copy().start()

    mine_spectra(1)

    def match_row(p, i):
        lane = iota((N, N), 1)
        row = iota((N, N), 0)
        low = lane < HALF
        found = dtile[...]
        top = HALF + i * N
        for j in range(SIDE):
            def at(rows, block):
                return ext[p, rows, block * N : block * N + N]

            def beside(rows, width):
                left, right = at(rows, j), at(rows, j + 2)
                return jnp.where(low[:width], right, left)

            centre = slice(top, top + N)
            above, below = slice(top - HALF, top), slice(top + N, top + N + HALF)
            dy, dx = off[0, p, i, j], off[1, p, i, j]
            in_rows = (row >= dy) & (row < dy + N)
            in_cols = (lane >= dx) & (lane < dx + N)
            main = jnp.where(in_cols, at(centre, j + 1), beside(centre, N))
            over = jnp.concatenate([at(below, j + 1), at(above, j + 1)], 0)
            over_side = jnp.concatenate([beside(below, HALF), beside(above, HALF)], 0)
            theirs = jnp.where(in_rows, main, jnp.where(in_cols, over, over_side))
            scores = inverse(cross(spec[9 * p + SIDE * i + j], forward(theirs, t)), t)
            peaks = peak(scores, dy, dx)
            for comp, (shift, by) in enumerate(zip(peaks, (dy, dx))):
                value = (by.astype(F32) + shift) * (1.0 / N)
                found = jnp.where((row8 == i) & (lane8 == 16 * (2 * comp + p) + j), value, found)
        dtile[...] = found

    dtile[...] = blank

    for p in (0, 1):
        for side in range(2):
            @pl.when(inside(p, 0, 1 - 2 * side))
            def _(p=p, side=side):
                col_rim(p, side).wait_recv()
        if p == 1:
            @pl.when(s < ns_ - 1)
            def _():
                tile_copy().wait_recv()
        for side in range(2):
            got = landed[p, side]
            column = slice(0, N) if side == 0 else slice(N + TILE, 2 * N + TILE)
            turned = swap(got)
            if side == 0:
                upper, lower = turned, got
            else:
                upper, lower = got, turned
            ext[p, HALF : HALF + TILE // 2, column] = upper
            ext[p, HALF + TILE // 2 : HALF + TILE, column] = lower
        match_row(p, 1)

    for p in (1, 0):
        for end in range(2):
            side = 1 - end
            @pl.when(inside(p, 1 - 2 * side, 0))
            def _(p=p, side=side):
                row_rim(p, side).wait_recv()

            for e in range(2):
                @pl.when(inside(p, 1 - 2 * side, 0) & inside(0, 0, 2 * e - 1))
                def _(p=p, end=end, e=e):
                    corner(p, end, e).start()
        for end in range(2):
            side = 1 - end
            for e in range(2):
                @pl.when(inside(p, 1 - 2 * side, 0) & inside(0, 0, 1 - 2 * e))
                def _(p=p, end=end, e=e):
                    corner(p, end, e).wait_recv()
            match_row(p, 2 * end)

    silent = (s == ns_ - 1) & ((lane8 & 16) != 0)
    found = jnp.where(silent, 0.0, dtile[...])
    dtile[...] = found

    def total_copy(k):
        return remote(dtile, dslots.at[s], ds.at[k], dr.at[s], (k, r, c))

    def total_arrival(k):
        return remote(dtile, dslots.at[k], ds.at[k], dr.at[k], (k, r, c))

    for k in range(ns_ - 1, 0, -1):
        @pl.when(k > s)
        def _(k=k):
            total_copy(k).start()
    for g in range(4):
        disp_ref[g // 2, g % 2] = (pltpu.roll(found, N - 16 * g, 1) if g else found)[0:SIDE, 0:SIDE]

    lane16 = iota((16, N), 1) & 15

    def frame(q):
        out = jnp.zeros((16, N), F32)
        for e in (-1, 0, 1):
            at = SIDE * (e + 1)
            by = (at - SIDE * q) % N
            strip = strips[e + 1]
            strip = pltpu.roll(strip, by, 1) if by else strip
            out = jnp.where((lane16 >= at) & (lane16 < at + SIDE), strip, out)
        return out

    def fill(centre, slots):
        for b in (-1, 0, 1):
            for e in (-1, 0, 1):
                at = SIDE * (b + 1)
                tile = centre[...] if (b, e) == (0, 0) else slots[3 * (b + 1) + e + 1]
                strips[e + 1, at : at + SIDE, :] = tile[0:SIDE]

    strips[...] = jnp.zeros_like(strips)
    for b, e in near:
        @pl.when(inside(0, b, e))
        def _(b=b, e=e):
            frame_copy(ptile, pslots, ps, pr, -b, -e).wait_recv()
    fill(ptile, pslots)
    v, right, down, anchor = (frame(q) for q in range(4))
    right_left = pltpu.roll(right, 1, 1)
    down_upper = pltpu.roll(down, 1, 0)

    for k in range(ns_ - 1):
        @pl.when(k < s)
        def _(k=k):
            total_arrival(k).wait_recv()
    lower = dslots[0]
    for k in range(1, ns_ - 1):
        lower = lower + dslots[k]
    second = (lane8 & 16) != 0
    below = lower + jnp.where(second, pltpu.roll(lower, 16, 1), pltpu.roll(lower, N - 16, 1))
    below = below + jnp.where(second, pltpu.roll(found, 16, 1), 0.0)
    ttile[...] = start - below
    for b, e in near:
        @pl.when(inside(0, b, e))
        def _(b=b, e=e):
            frame_copy(ttile, tslots, ns, nr, b, e).start()

    for p in (0, 1):
        for side in range(2):
            @pl.when(inside(-p, 0, 2 * side - 1))
            def _(p=p, side=side):
                col_rim(p, side).wait_send()

            @pl.when(inside(-p, 2 * side - 1, 0))
            def _(p=p, side=side):
                row_rim(p, side).wait_send()

            for e in range(2):
                @pl.when(inside(p, 2 * side - 1, 0) & inside(0, 0, 2 * e - 1))
                def _(p=p, side=side, e=e):
                    corner(p, side, e).wait_send()

    @pl.when(s > 0)
    def _():
        tile_copy().wait_send()

    for k in range(1, ns_):
        @pl.when(k > s)
        def _(k=k):
            total_copy(k).wait_send()
    for b, e in near:
        @pl.when(inside(0, b, e))
        def _(b=b, e=e):
            frame_copy(ptile, pslots, ps, pr, b, e).wait_send()
            frame_copy(ttile, tslots, ns, nr, b, e).wait_send()
            frame_copy(ttile, tslots, ns, nr, -b, -e).wait_recv()

    fill(ttile, tslots)
    target = frame(0)
    for _ in range(ITERS):
        v = (
            v
            + right * (pltpu.roll(v, N - 1, 1) - v)
            + right_left * (pltpu.roll(v, 1, 1) - v)
            + down * (pltpu.roll(v, 15, 0) - v)
            + down_upper * (pltpu.roll(v, 1, 0) - v)
            + anchor * (target - v)
        )
    v = pltpu.roll(v, 16 - SIDE, 0)
    for g in range(4):
        warped_ref[g // 2, g % 2] = pltpu.roll(v, (N - 16 * g - SIDE) % N, 1)[0:SIDE, 0:SIDE]


def per_device(sizes, images, offsets, warp, stiffness, valid):
    vmem = pl.BlockSpec(memory_space=pltpu.VMEM)
    dma = pltpu.SemaphoreType.DMA
    out = jax.ShapeDtypeStruct((2, 2, SIDE, SIDE), F32)
    n = sizes[0]
    return pl.pallas_call(
        functools.partial(kernel, sizes),
        name="align",
        out_shape=(out, out),
        in_specs=[pl.BlockSpec(memory_space=pl.ANY), pl.BlockSpec(memory_space=pltpu.SMEM)] + [vmem] * 11,
        out_specs=(vmem, vmem),
        scratch_shapes=[
            pltpu.VMEM((TILE, TILE), F32),
            pltpu.VMEM((2, TILE + 2 * HALF, TILE + 2 * N), F32),
            pltpu.VMEM((18, N, N), F32),
            pltpu.VMEM((2, 2, TILE // 2, N), F32),
            pltpu.VMEM((2, 2, TILE // 2, N), F32),
            pltpu.VMEM((10, 8, N), F32),
            pltpu.VMEM((8, N), F32),
            pltpu.VMEM((9, 8, N), F32),
            pltpu.VMEM((8, N), F32),
            pltpu.VMEM((9, 8, N), F32),
            pltpu.VMEM((8, N), F32),
            pltpu.VMEM((n, 8, N), F32),
            pltpu.VMEM((3, 16, N), F32),
            dma((2,)),
            dma((1,)),
            dma((1,)),
            dma((4,)),
            dma((4,)),
            dma((4,)),
            dma((4,)),
            dma((8,)),
            dma((8,)),
            dma((9,)),
            dma((9,)),
            dma((n,)),
            dma((n,)),
            dma((9,)),
            dma((9,)),
        ],
        compiler_params=pltpu.CompilerParams(
            collective_id=0, has_side_effects=True, vmem_limit_bytes=32 * 1024 * 1024
        ),
    )(images, offsets, warp, stiffness, valid, *(jnp.asarray(a) for a in tables()))


def solution(mesh):
    sizes = tuple(mesh.shape[a] for a in ("sec", "row", "col"))
    return jax.shard_map(
        functools.partial(per_device, sizes),
        mesh=mesh,
        in_specs=(
            P("sec", "row", "col"),
            P(None, "sec", "row", "col"),
            P(None, "sec", "row", "col"),
            P(None, "sec", "row", "col"),
            P("sec", "row", "col"),
        ),
        out_specs=(P(None, "sec", "row", "col"), P(None, "sec", "row", "col")),
        check_vma=False,
    )
```

```python
import functools

import jax
import jax.numpy as jnp
import ml_dtypes
import numpy as np
from jax import lax
from jax.experimental import pallas as pl
from jax.experimental.pallas import tpu as pltpu
from jax.sharding import PartitionSpec as P

MESH = pl.DeviceIdType.MESH
N = 128
HALF = 64
SIDE = 3
TILE = SIDE * N
BLOCKS = 2 * TILE // N
SHARPNESS = 80.0
ANCHOR = 0.2
ITERS = 3
BF = jnp.bfloat16
F32 = jnp.float32


def split3(a):
    high = a.astype(ml_dtypes.bfloat16)
    rest = a - high.astype(np.float64)
    mid = rest.astype(ml_dtypes.bfloat16)
    low = (rest - mid.astype(np.float64)).astype(ml_dtypes.bfloat16)
    return high, mid, low


def tables():
    x = np.arange(N)
    forward = np.zeros((N, N))
    for f in range(HALF):
        forward[f] = np.cos(2 * np.pi * ((f * x) % N) / N)
    forward[HALF] = 1 - 2 * (x % 2)
    for f in range(1, HALF):
        forward[HALF + f] = np.sin(2 * np.pi * ((f * x) % N) / N)
    scale = np.full(N, 2.0 / N)
    scale[0] = scale[HALF] = 1.0 / N
    inverse = (forward * scale[:, None]).T

    def right(a):
        h, m, l = split3(a)
        return np.block([[h, m], [h, m]]), np.concatenate([h, l], 0)

    return np.concatenate([*right(forward.T), *right(inverse.T * np.sqrt(SHARPNESS / (N * N)))], 1)


def parts(x):
    high = x.astype(BF)
    rest = x - high.astype(F32)
    mid = rest.astype(BF)
    low = (rest - mid.astype(F32)).astype(BF)
    return high, mid, low


def dot(a, b):
    return jnp.dot(a, b, preferred_element_type=F32)


def right_mul(x, wa, wb):
    high, mid, low = parts(x)
    a = dot(jnp.concatenate([high, mid], 1), wa)
    return a[:, :N] + a[:, N:] + dot(jnp.concatenate([low, high], 1), wb)


def turn(x):
    return jnp.concatenate([x[k : k + N].T for k in range(0, x.shape[0], N)], 0)


def forward(x, t):
    return right_mul(turn(right_mul(x, t[:, 0 : 2 * N], t[:, 2 * N : 3 * N])), t[:, 0 : 2 * N], t[:, 2 * N : 3 * N])


def inverse(x, t):
    return right_mul(turn(right_mul(x, t[:, 3 * N : 5 * N], t[:, 5 * N :])), t[:, 3 * N : 5 * N], t[:, 5 * N :])


def iota(shape, dim):
    return lax.broadcasted_iota(jnp.int32, shape, dim)


def swap(x):
    return pltpu.roll(x, HALF, 1)


def cross(mine, theirs):
    lane = iota((N, N), 1)
    single = (lane & (HALF - 1)) == 0
    turned = swap(theirs)
    first = jnp.where(single | (lane < HALF), theirs, -turned)
    second = jnp.where(single, 0.0, jnp.where(lane < HALF, turned, theirs))
    other = swap(mine)
    even, odd = slice(0, HALF), slice(HALF, N)

    def pair(a, b):
        return mine[a] * first[b] + other[a] * second[b]

    lone = iota((HALF, N), 0) == 0
    both = pair(odd, odd)
    top = pair(even, even) + jnp.where(lone, 0.0, both)
    top = jnp.where(lone & (iota((HALF, N), 1) == 0), 0.0, top)
    low = jnp.where(lone, both, pair(even, odd) - pair(odd, even))
    return jnp.concatenate([top, low], 0)


def peaks(scores, shifts):
    count = len(shifts)
    blocks = [scores[k * N : k * N + N] for k in range(count)]
    highest = jnp.concatenate([jnp.max(x, axis=0, keepdims=True) for x in blocks], 0)
    highest = jnp.max(highest, axis=1, keepdims=True)
    sums = []
    for k, (dy, dx) in enumerate(shifts):
        rows = (((iota((N, N), 0) - dy + HALF) & (N - 1)) - HALF).astype(F32)
        cols = (((iota((1, N), 1) - dx + HALF) & (N - 1)) - HALF).astype(F32)
        weights = jnp.exp(blocks[k] - highest[k : k + 1])
        by_col = jnp.sum(weights, axis=0, keepdims=True)
        sums.append((by_col, jnp.sum(weights * rows, axis=0, keepdims=True), by_col * cols))
    sums = [jnp.sum(jnp.concatenate([x[q] for x in sums], 0), axis=1, keepdims=True) for q in range(3)]
    return sums[1] / sums[0], sums[2] / sums[0]


def kernel(sizes, images, off, warp, stiff, valid, table, disp_ref, warped_ref, *rest):
    (t, own, ext, spec, packed, landed, small, ptile, pslots, ttile, tslots, dtile, dslots, strips) = rest[:14]
    lsem, ts, tr, rs, rr, cs, cr, ks, kr, ps, pr, ds, dr, ns, nr = rest[14:]
    ns_, nr_, nc_ = sizes
    s, r, c = lax.axis_index("sec"), lax.axis_index("row"), lax.axis_index("col")

    def inside(a, b, e):
        ok = None
        for at, by, n in ((s, a, ns_), (r, b, nr_), (c, e, nc_)):
            if by:
                here = (at + by >= 0) & (at + by < n)
                ok = here if ok is None else ok & here
        return ok

    def there(a, b, e):
        return (s + a, r + b, c + e)

    locals_ = [
        pltpu.make_async_copy(images.at[0], own, lsem.at[0]),
        pltpu.make_async_copy(images.at[1], ext.at[0, HALF : HALF + TILE, N : N + TILE], lsem.at[1]),
        pltpu.make_async_copy(table, t, lsem.at[2]),
    ]
    for copy in locals_:
        copy.start()

    near = [(a, b) for a in (-1, 0, 1) for b in (-1, 0, 1) if (a, b) != (0, 0)]
    sides = [(-1, 0), (1, 0), (0, -1), (0, 1)]
    goes = [(k, 0, 0) for k in range(1, ns_)] + [(-1, 0, 0)] + [(-1, b, e) for b, e in sides] + [(0, b, e) for b, e in near]
    barrier = pltpu.get_barrier_semaphore()
    expected = 0
    for a, b, e in goes:
        @pl.when(inside(-a, -b, -e))
        def _(a=a, b=b, e=e):
            pl.semaphore_signal(barrier, inc=1, device_id=there(-a, -b, -e), device_id_type=MESH)

        expected = expected + inside(a, b, e).astype(jnp.int32)

    @pl.when(r == 0)
    def _():
        for p in range(2):
            ext[p, 0:HALF, :] = jnp.zeros((HALF, TILE + 2 * N), F32)

    @pl.when(r == nr_ - 1)
    def _():
        for p in range(2):
            ext[p, HALF + TILE :, :] = jnp.zeros((HALF, TILE + 2 * N), F32)

    @pl.when(c == 0)
    def _():
        for p in range(2):
            ext[p, 0:HALF, 0:N] = jnp.zeros((HALF, N), F32)
            ext[p, HALF + TILE :, 0:N] = jnp.zeros((HALF, N), F32)
            landed[p, 0] = jnp.zeros((TILE // 2, N), F32)

    @pl.when(c == nc_ - 1)
    def _():
        for p in range(2):
            ext[p, 0:HALF, N + TILE :] = jnp.zeros((HALF, N), F32)
            ext[p, HALF + TILE :, N + TILE :] = jnp.zeros((HALF, N), F32)
            landed[p, 1] = jnp.zeros((TILE // 2, N), F32)

    @pl.when(s == ns_ - 1)
    def _():
        ext[1] = jnp.zeros((TILE + 2 * HALF, TILE + 2 * N), F32)
        landed[1] = jnp.zeros((2, TILE // 2, N), F32)

    blank = jnp.zeros((8, N), F32)
    for b, e in near:
        @pl.when(jnp.logical_not(inside(0, b, e)))
        def _(b=b, e=e):
            pslots[3 * (b + 1) + e + 1] = blank
            tslots[3 * (b + 1) + e + 1] = blank

    for k in range(ns_):
        @pl.when(s <= k)
        def _(k=k):
            dslots[k] = blank

    row8, lane8 = iota((8, N), 0), iota((8, N), 1)
    small[...] = jnp.zeros_like(small)
    for comp in range(2):
        for sec in range(2):
            small[2 * comp + sec, 0:SIDE, 0:SIDE] = warp[comp, :, sec]
            small[4 + 2 * comp + sec, 0:SIDE, 0:SIDE] = stiff[comp, :, sec]
    for sec in range(2):
        small[8 + sec, 0:SIDE, 0:SIDE] = ANCHOR * valid[:, sec].astype(F32)
    start = jnp.zeros((8, N), F32)
    held = jnp.zeros((8, N), F32)
    for g in range(4):
        sec = g % 2
        w = small[g]
        right = jnp.where((c == nc_ - 1) & (lane8 == SIDE - 1), 0.0, small[4 + sec])
        down = jnp.where((r == nr_ - 1) & (row8 == SIDE - 1), 0.0, small[6 + sec])
        start = start + (pltpu.roll(w, 16 * g, 1) if g else w)
        for q, quantity in enumerate((w, right, down, small[8 + sec])):
            by = 16 * g + SIDE * q
            held = held + (pltpu.roll(quantity, by, 1) if by else quantity)
    ptile[...] = held

    for copy in locals_:
        copy.wait()

    low_lane = iota((TILE // 2, N), 1) < HALF
    for im in range(2):
        for side in range(2):
            if im == 0:
                strip = own[:, 0:N] if side == 0 else own[:, TILE - N :]
            else:
                strip = ext[0, HALF : HALF + TILE, N : 2 * N] if side == 0 else ext[0, HALF : HALF + TILE, TILE : TILE + N]
            upper, lower = strip[: TILE // 2], strip[TILE // 2 :]
            packed[im, side] = jnp.where(low_lane, upper, swap(lower)) if side == 0 else jnp.where(low_lane, swap(upper), lower)

    def mine_spectra(p):
        def step(i, _):
            at = pl.multiple_of(i * N, N)
            if p == 0:
                blocks = [own[pl.ds(at, N), j * N : j * N + N] for j in range(SIDE)]
            else:
                at = pl.multiple_of(at + HALF, HALF)
                blocks = [ext[0, pl.ds(at, N), j * N + N : j * N + 2 * N] for j in range(SIDE)]
            found = forward(jnp.concatenate(blocks, 0), t)
            for j in range(SIDE):
                spec[9 * p + SIDE * i + j] = found[j * N : j * N + N]
            return 0

        lax.fori_loop(0, SIDE, step, 0)

    mine_spectra(0)

    pl.semaphore_wait(barrier, expected)

    def remote(src, dst, send, recv, target):
        return pltpu.make_async_remote_copy(
            src_ref=src, dst_ref=dst, send_sem=send, recv_sem=recv, device_id=target, device_id_type=MESH
        )

    def col_rim(p, side):
        e = 2 * side - 1
        return remote(
            packed.at[1 - p, side], landed.at[p, 1 - side], cs.at[2 * p + side], cr.at[2 * p + 1 - side], there(-p, 0, e)
        )

    def row_rim(p, side):
        b = 2 * side - 1
        src = images.at[1 - p, TILE - HALF : TILE, :] if side else images.at[1 - p, 0:HALF, :]
        at = slice(0, HALF) if side else slice(HALF + TILE, 2 * HALF + TILE)
        return remote(src, ext.at[p, at, N : N + TILE], rs.at[2 * p + side], rr.at[2 * p + 1 - side], there(-p, b, 0))

    def corner(p, end, side):
        e = 2 * side - 1
        at = slice(HALF + TILE, 2 * HALF + TILE) if end else slice(0, HALF)
        src = slice(TILE, TILE + N) if side else slice(N, 2 * N)
        dst = slice(0, N) if side else slice(N + TILE, 2 * N + TILE)
        n = 4 * p + 2 * end
        return remote(ext.at[p, at, src], ext.at[p, at, dst], ks.at[n + side], kr.at[n + 1 - side], there(0, 0, e))

    def tile_copy():
        return remote(images.at[0], ext.at[1, HALF : HALF + TILE, N : N + TILE], ts.at[0], tr.at[0], there(-1, 0, 0))

    def frame_copy(src, slots, send, recv, b, e):
        n, m = 3 * (b + 1) + e + 1, 3 * (1 - b) + 1 - e
        return remote(src, slots.at[m], send.at[n], recv.at[m], there(0, b, e))

    for b, e in near:
        @pl.when(inside(0, b, e))
        def _(b=b, e=e):
            frame_copy(ptile, pslots, ps, pr, b, e).start()

    for p in (0, 1):
        for side in range(2):
            @pl.when(inside(-p, 0, 2 * side - 1))
            def _(p=p, side=side):
                col_rim(p, side).start()
    for p in (1, 0):
        for side in range(2):
            @pl.when(inside(-p, 2 * side - 1, 0))
            def _(p=p, side=side):
                row_rim(p, side).start()

    @pl.when(s > 0)
    def _():
        tile_copy().start()

    mine_spectra(1)

    def match_row(p, i):
        lane = iota((N, N), 1)
        row = iota((N, N), 0)
        low = lane < HALF
        found = dtile[...]
        stack = []
        top = HALF + i * N
        for j in range(SIDE):
            def at(rows, block):
                return ext[p, rows, block * N : block * N + N]

            def beside(rows, width):
                left, right = at(rows, j), at(rows, j + 2)
                return jnp.where(low[:width], right, left)

            centre = slice(top, top + N)
            above, below = slice(top - HALF, top), slice(top + N, top + N + HALF)
            dy, dx = off[0, i, p, j], off[1, i, p, j]
            in_rows = (row >= dy) & (row < dy + N)
            in_cols = (lane >= dx) & (lane < dx + N)
            main = jnp.where(in_cols, at(centre, j + 1), beside(centre, N))
            over = jnp.concatenate([at(below, j + 1), at(above, j + 1)], 0)
            over_side = jnp.concatenate([beside(below, HALF), beside(above, HALF)], 0)
            stack.append(jnp.where(in_rows, main, jnp.where(in_cols, over, over_side)))
        theirs = forward(jnp.concatenate(stack, 0), t)
        scores = inverse(
            jnp.concatenate([cross(spec[9 * p + SIDE * i + j], theirs[j * N : j * N + N]) for j in range(SIDE)], 0), t
        )
        shifts = [(off[0, i, p, j], off[1, i, p, j]) for j in range(SIDE)]
        for comp, found_shifts in enumerate(peaks(scores, shifts)):
            for j in range(SIDE):
                value = (shifts[j][comp].astype(F32) + found_shifts[j : j + 1]) * (1.0 / N)
                found = jnp.where((row8 == i) & (lane8 == 16 * (2 * comp + p) + j), value, found)
        dtile[...] = found

    dtile[...] = blank

    for p in (0, 1):
        for side in range(2):
            @pl.when(inside(p, 0, 1 - 2 * side))
            def _(p=p, side=side):
                col_rim(p, side).wait_recv()
        if p == 1:
            @pl.when(s < ns_ - 1)
            def _():
                tile_copy().wait_recv()
        for side in range(2):
            got = landed[p, side]
            column = slice(0, N) if side == 0 else slice(N + TILE, 2 * N + TILE)
            turned = swap(got)
            if side == 0:
                upper, lower = turned, got
            else:
                upper, lower = got, turned
            ext[p, HALF : HALF + TILE // 2, column] = upper
            ext[p, HALF + TILE // 2 : HALF + TILE, column] = lower
        match_row(p, 1)

    for p in (1, 0):
        for end in range(2):
            side = 1 - end
            @pl.when(inside(p, 1 - 2 * side, 0))
            def _(p=p, side=side):
                row_rim(p, side).wait_recv()

            for e in range(2):
                @pl.when(inside(p, 1 - 2 * side, 0) & inside(0, 0, 2 * e - 1))
                def _(p=p, end=end, e=e):
                    corner(p, end, e).start()
        for end in range(2):
            side = 1 - end
            for e in range(2):
                @pl.when(inside(p, 1 - 2 * side, 0) & inside(0, 0, 1 - 2 * e))
                def _(p=p, end=end, e=e):
                    corner(p, end, e).wait_recv()
            match_row(p, 2 * end)

    silent = (s == ns_ - 1) & ((lane8 & 16) != 0)
    found = jnp.where(silent, 0.0, dtile[...])
    dtile[...] = found

    def total_copy(k):
        return remote(dtile, dslots.at[s], ds.at[k], dr.at[s], (k, r, c))

    def total_arrival(k):
        return remote(dtile, dslots.at[k], ds.at[k], dr.at[k], (k, r, c))

    for k in range(ns_ - 1, 0, -1):
        @pl.when(k > s)
        def _(k=k):
            total_copy(k).start()
    for g in range(4):
        disp_ref[g // 2, :, g % 2] = (pltpu.roll(found, N - 16 * g, 1) if g else found)[0:SIDE, 0:SIDE]

    lane16 = iota((16, N), 1) & 15

    def frame(q):
        out = jnp.zeros((16, N), F32)
        for e in (-1, 0, 1):
            at = SIDE * (e + 1)
            by = (at - SIDE * q) % N
            strip = strips[e + 1]
            strip = pltpu.roll(strip, by, 1) if by else strip
            out = jnp.where((lane16 >= at) & (lane16 < at + SIDE), strip, out)
        return out

    def fill(centre, slots):
        for b in (-1, 0, 1):
            for e in (-1, 0, 1):
                at = SIDE * (b + 1)
                tile = centre[...] if (b, e) == (0, 0) else slots[3 * (b + 1) + e + 1]
                strips[e + 1, at : at + SIDE, :] = tile[0:SIDE]

    strips[...] = jnp.zeros_like(strips)
    for b, e in near:
        @pl.when(inside(0, b, e))
        def _(b=b, e=e):
            frame_copy(ptile, pslots, ps, pr, -b, -e).wait_recv()
    fill(ptile, pslots)
    v, right, down, anchor = (frame(q) for q in range(4))
    right_left = pltpu.roll(right, 1, 1)
    down_upper = pltpu.roll(down, 1, 0)

    for k in range(ns_ - 1):
        @pl.when(k < s)
        def _(k=k):
            total_arrival(k).wait_recv()
    lower = dslots[0]
    for k in range(1, ns_ - 1):
        lower = lower + dslots[k]
    second = (lane8 & 16) != 0
    below = lower + jnp.where(second, pltpu.roll(lower, 16, 1), pltpu.roll(lower, N - 16, 1))
    below = below + jnp.where(second, pltpu.roll(found, 16, 1), 0.0)
    ttile[...] = start - below
    for b, e in near:
        @pl.when(inside(0, b, e))
        def _(b=b, e=e):
            frame_copy(ttile, tslots, ns, nr, b, e).start()

    for p in (0, 1):
        for side in range(2):
            @pl.when(inside(-p, 0, 2 * side - 1))
            def _(p=p, side=side):
                col_rim(p, side).wait_send()

            @pl.when(inside(-p, 2 * side - 1, 0))
            def _(p=p, side=side):
                row_rim(p, side).wait_send()

            for e in range(2):
                @pl.when(inside(p, 2 * side - 1, 0) & inside(0, 0, 2 * e - 1))
                def _(p=p, side=side, e=e):
                    corner(p, side, e).wait_send()

    @pl.when(s > 0)
    def _():
        tile_copy().wait_send()

    for k in range(1, ns_):
        @pl.when(k > s)
        def _(k=k):
            total_copy(k).wait_send()
    for b, e in near:
        @pl.when(inside(0, b, e))
        def _(b=b, e=e):
            frame_copy(ptile, pslots, ps, pr, b, e).wait_send()
            frame_copy(ttile, tslots, ns, nr, b, e).wait_send()
            frame_copy(ttile, tslots, ns, nr, -b, -e).wait_recv()

    fill(ttile, tslots)
    target = frame(0)
    for _ in range(ITERS):
        v = (
            v
            + right * (pltpu.roll(v, N - 1, 1) - v)
            + right_left * (pltpu.roll(v, 1, 1) - v)
            + down * (pltpu.roll(v, 15, 0) - v)
            + down_upper * (pltpu.roll(v, 1, 0) - v)
            + anchor * (target - v)
        )
    v = pltpu.roll(v, 16 - SIDE, 0)
    for g in range(4):
        warped_ref[g // 2, :, g % 2] = pltpu.roll(v, (N - 16 * g - SIDE) % N, 1)[0:SIDE, 0:SIDE]


def per_device(sizes, images, offsets, warp, stiffness, valid):
    vmem = pl.BlockSpec(memory_space=pltpu.VMEM)
    anywhere = pl.BlockSpec(memory_space=pl.ANY)
    dma = pltpu.SemaphoreType.DMA
    out = jax.ShapeDtypeStruct((2, SIDE, 2, SIDE), F32)
    n = sizes[0]
    turned = (0, 2, 1, 3)
    outs = pl.pallas_call(
        functools.partial(kernel, sizes),
        name="align",
        out_shape=(out, out),
        in_specs=[anywhere, pl.BlockSpec(memory_space=pltpu.SMEM), vmem, vmem, vmem, anywhere],
        out_specs=(vmem, vmem),
        scratch_shapes=[
            pltpu.VMEM((2 * N, 6 * N), BF),
            pltpu.VMEM((TILE, TILE), F32),
            pltpu.VMEM((2, TILE + 2 * HALF, TILE + 2 * N), F32),
            pltpu.VMEM((18, N, N), F32),
            pltpu.VMEM((2, 2, TILE // 2, N), F32),
            pltpu.VMEM((2, 2, TILE // 2, N), F32),
            pltpu.VMEM((10, 8, N), F32),
            pltpu.VMEM((8, N), F32),
            pltpu.VMEM((9, 8, N), F32),
            pltpu.VMEM((8, N), F32),
            pltpu.VMEM((9, 8, N), F32),
            pltpu.VMEM((8, N), F32),
            pltpu.VMEM((n, 8, N), F32),
            pltpu.VMEM((3, 16, N), F32),
            dma((3,)),
            dma((1,)),
            dma((1,)),
            dma((4,)),
            dma((4,)),
            dma((4,)),
            dma((4,)),
            dma((8,)),
            dma((8,)),
            dma((9,)),
            dma((9,)),
            dma((n,)),
            dma((n,)),
            dma((9,)),
            dma((9,)),
        ],
        compiler_params=pltpu.CompilerParams(
            collective_id=0, has_side_effects=True, vmem_limit_bytes=60 * 1024 * 1024
        ),
    )(
        images,
        offsets.transpose(turned),
        warp.transpose(turned),
        stiffness.transpose(turned),
        valid.transpose(1, 0, 2),
        jnp.asarray(tables()),
    )
    return tuple(x.transpose(turned) for x in outs)


def solution(mesh):
    sizes = tuple(mesh.shape[a] for a in ("sec", "row", "col"))
    return jax.shard_map(
        functools.partial(per_device, sizes),
        mesh=mesh,
        in_specs=(
            P("sec", "row", "col"),
            P(None, "sec", "row", "col"),
            P(None, "sec", "row", "col"),
            P(None, "sec", "row", "col"),
            P("sec", "row", "col"),
        ),
        out_specs=(P(None, "sec", "row", "col"), P(None, "sec", "row", "col")),
        check_vma=False,
    )
```

```python
import functools

import jax
import jax.numpy as jnp
import ml_dtypes
import numpy as np
from jax import lax
from jax.experimental import pallas as pl
from jax.experimental.pallas import tpu as pltpu
from jax.sharding import PartitionSpec as P

MESH = pl.DeviceIdType.MESH
N = 128
HALF = 64
SIDE = 3
TILE = SIDE * N
BLOCKS = 2 * TILE // N
SHARPNESS = 80.0
ANCHOR = 0.2
ITERS = 3
LEGS = 4
PARTS = (2, 4)
BF = jnp.bfloat16
F32 = jnp.float32


def split3(a):
    high = a.astype(ml_dtypes.bfloat16)
    rest = a - high.astype(np.float64)
    mid = rest.astype(ml_dtypes.bfloat16)
    low = (rest - mid.astype(np.float64)).astype(ml_dtypes.bfloat16)
    return high, mid, low


def tables():
    x = np.arange(N)
    forward = np.zeros((N, N))
    for f in range(HALF):
        forward[f] = np.cos(2 * np.pi * ((f * x) % N) / N)
    forward[HALF] = 1 - 2 * (x % 2)
    for f in range(1, HALF):
        forward[HALF + f] = np.sin(2 * np.pi * ((f * x) % N) / N)
    scale = np.full(N, 2.0 / N)
    scale[0] = scale[HALF] = 1.0 / N
    inverse = (forward * scale[:, None]).T

    def right(a):
        h, m, l = split3(a)
        return np.block([[h, m], [h, m]]), np.concatenate([h, l], 0)

    return np.concatenate([*right(forward.T), *right(inverse.T * np.sqrt(SHARPNESS / (N * N)))], 1)


def parts(x):
    high = x.astype(BF)
    rest = x - high.astype(F32)
    mid = rest.astype(BF)
    low = (rest - mid.astype(F32)).astype(BF)
    return high, mid, low


def dot(a, b):
    return jnp.dot(a, b, preferred_element_type=F32)


def right_mul(x, wa, wb):
    high, mid, low = parts(x)
    a = dot(jnp.concatenate([high, mid], 1), wa)
    return a[:, :N] + a[:, N:] + dot(jnp.concatenate([low, high], 1), wb)


def turn(x):
    return jnp.concatenate([x[k : k + N].T for k in range(0, x.shape[0], N)], 0)


def forward(x, t):
    return right_mul(turn(right_mul(x, t[:, 0 : 2 * N], t[:, 2 * N : 3 * N])), t[:, 0 : 2 * N], t[:, 2 * N : 3 * N])


def inverse(x, t):
    return right_mul(turn(right_mul(x, t[:, 3 * N : 5 * N], t[:, 5 * N :])), t[:, 3 * N : 5 * N], t[:, 5 * N :])


def iota(shape, dim):
    return lax.broadcasted_iota(jnp.int32, shape, dim)


def swap(x):
    return pltpu.roll(x, HALF, 1)


def cross(mine, theirs):
    lane = iota((N, N), 1)
    single = (lane & (HALF - 1)) == 0
    turned = swap(theirs)
    first = jnp.where(single | (lane < HALF), theirs, -turned)
    second = jnp.where(single, 0.0, jnp.where(lane < HALF, turned, theirs))
    other = swap(mine)
    even, odd = slice(0, HALF), slice(HALF, N)

    def pair(a, b):
        return mine[a] * first[b] + other[a] * second[b]

    lone = iota((HALF, N), 0) == 0
    both = pair(odd, odd)
    top = pair(even, even) + jnp.where(lone, 0.0, both)
    top = jnp.where(lone & (iota((HALF, N), 1) == 0), 0.0, top)
    low = jnp.where(lone, both, pair(even, odd) - pair(odd, even))
    return jnp.concatenate([top, low], 0)


def peaks(scores, shifts):
    count = len(shifts)
    blocks = [scores[k * N : k * N + N] for k in range(count)]
    highest = jnp.concatenate([jnp.max(x, axis=0, keepdims=True) for x in blocks], 0)
    highest = jnp.max(highest, axis=1, keepdims=True)
    sums = []
    for k, (dy, dx) in enumerate(shifts):
        rows = (((iota((N, N), 0) - dy + HALF) & (N - 1)) - HALF).astype(F32)
        cols = (((iota((1, N), 1) - dx + HALF) & (N - 1)) - HALF).astype(F32)
        weights = jnp.exp(blocks[k] - highest[k : k + 1])
        by_col = jnp.sum(weights, axis=0, keepdims=True)
        sums.append((by_col, jnp.sum(weights * rows, axis=0, keepdims=True), by_col * cols))
    sums = [jnp.sum(jnp.concatenate([x[q] for x in sums], 0), axis=1, keepdims=True) for q in range(3)]
    return sums[1] / sums[0], sums[2] / sums[0]


def kernel(sizes, images, off, warp, stiff, valid, table, disp_ref, warped_ref, *rest):
    (t, own, ext, spec, packed, landed, transit, small, ftile, fslots, dtile, dslots, strips) = rest[:13]
    lsem, ts, tr, rs, rr, cs, cr, ks, kr, ds, dr, fs, fr = rest[13:]
    ns_, nr_, nc_ = sizes
    ny_, nz_ = nr_ // 2, 2 * nc_
    hop = nc_ // LEGS
    s, r, c = lax.axis_index("sec"), lax.axis_index("row"), lax.axis_index("col")
    y, half = r // 2, lax.rem(r, 2)
    z = half * nc_ + c

    def inside(a, b, e):
        ok = None
        for at, by, n in ((s, a, ns_), (r, b, nr_), (c, e, nc_)):
            if by:
                here = (at + by >= 0) & (at + by < n)
                ok = here if ok is None else ok & here
        return ok

    def there(a, b, e):
        return (s + a, r + b, c + e)

    def on_line(a, to_y, to_z):
        to_z = lax.rem(to_z + 2 * nz_, nz_)
        return (s + a, 2 * to_y + to_z // nc_, lax.rem(to_z, nc_))

    def half_at(at_z):
        return lax.rem(at_z + 2 * nz_, nz_) // nc_

    locals_ = [
        pltpu.make_async_copy(images.at[0], own, lsem.at[0]),
        pltpu.make_async_copy(images.at[1], ext.at[0, HALF : HALF + TILE, N : N + TILE], lsem.at[1]),
        pltpu.make_async_copy(table, t, lsem.at[2]),
    ]
    for copy in locals_:
        copy.start()

    barrier = pltpu.get_barrier_semaphore()
    goes = [(k, 0, 0) for k in range(1, ns_)] + [(-1, 0, 0), (-1, 0, -1), (-1, 0, 1), (0, 0, -1), (0, 0, 1)]
    expected = 0
    for a, b, e in goes:
        @pl.when(inside(-a, -b, -e))
        def _(a=a, b=b, e=e):
            pl.semaphore_signal(barrier, inc=1, device_id=there(-a, -b, -e), device_id_type=MESH)

        expected = expected + inside(a, b, e).astype(jnp.int32)
    for a, e in ((0, hop), (0, -hop), (-1, -hop)):
        for b in (-1, 0, 1):
            def both(sign, a=a, b=b):
                return (s + sign * a >= 0) & (s + sign * a < ns_) & (y + sign * b >= 0) & (y + sign * b < ny_)

            @pl.when(both(-1))
            def _(a=a, b=b, e=e):
                pl.semaphore_signal(barrier, inc=1, device_id=on_line(-a, y - b, z - e), device_id_type=MESH)

            expected = expected + both(1).astype(jnp.int32)

    @pl.when(r == 0)
    def _():
        for p in range(2):
            ext[p, 0:HALF, :] = jnp.zeros((HALF, TILE + 2 * N), F32)

    @pl.when(r == nr_ - 1)
    def _():
        for p in range(2):
            ext[p, HALF + TILE :, :] = jnp.zeros((HALF, TILE + 2 * N), F32)

    @pl.when(c == 0)
    def _():
        for p in range(2):
            ext[p, 0:HALF, 0:N] = jnp.zeros((HALF, N), F32)
            ext[p, HALF + TILE :, 0:N] = jnp.zeros((HALF, N), F32)
            landed[p, 0] = jnp.zeros((TILE // 2, N), F32)

    @pl.when(c == nc_ - 1)
    def _():
        for p in range(2):
            ext[p, 0:HALF, N + TILE :] = jnp.zeros((HALF, N), F32)
            ext[p, HALF + TILE :, N + TILE :] = jnp.zeros((HALF, N), F32)
            landed[p, 1] = jnp.zeros((TILE // 2, N), F32)

    @pl.when(s == ns_ - 1)
    def _():
        ext[1] = jnp.zeros((TILE + 2 * HALF, TILE + 2 * N), F32)
        landed[1] = jnp.zeros((2, TILE // 2, N), F32)

    near = [(b, e) for b in (-1, 0, 1) for e in (-1, 0, 1) if (b, e) != (0, 0)]
    blank = jnp.zeros((8, N), F32)
    for b, e in near:
        @pl.when(jnp.logical_not(inside(0, b, e)))
        def _(b=b, e=e):
            fslots[3 * (b + 1) + e + 1] = blank

    for k in range(ns_):
        @pl.when(s <= k)
        def _(k=k):
            dslots[k] = blank

    row8, lane8 = iota((8, N), 0), iota((8, N), 1)
    small[...] = jnp.zeros_like(small)
    for comp in range(2):
        for sec in range(2):
            small[2 * comp + sec, 0:SIDE, 0:SIDE] = warp[comp, :, sec]
            small[4 + 2 * comp + sec, 0:SIDE, 0:SIDE] = stiff[comp, :, sec]
    for sec in range(2):
        small[8 + sec, 0:SIDE, 0:SIDE] = ANCHOR * valid[:, sec].astype(F32)
    start = jnp.zeros((8, N), F32)
    held = jnp.zeros((8, N), F32)
    for g in range(4):
        sec = g % 2
        w = small[g]
        right = jnp.where((c == nc_ - 1) & (lane8 == SIDE - 1), 0.0, small[4 + sec])
        down = jnp.where((r == nr_ - 1) & (row8 == SIDE - 1), 0.0, small[6 + sec])
        start = start + (pltpu.roll(w, 16 * g, 1) if g else w)
        for q, quantity in enumerate((w, right, down, small[8 + sec])):
            by = 16 * g + SIDE * q
            held = held + (pltpu.roll(quantity, by, 1) if by else quantity)

    for copy in locals_:
        copy.wait()

    low_lane = iota((TILE // 2, N), 1) < HALF
    for im in range(2):
        for side in range(2):
            if im == 0:
                strip = own[:, 0:N] if side == 0 else own[:, TILE - N :]
            else:
                strip = ext[0, HALF : HALF + TILE, N : 2 * N] if side == 0 else ext[0, HALF : HALF + TILE, TILE : TILE + N]
            upper, lower = strip[: TILE // 2], strip[TILE // 2 :]
            packed[im, side] = jnp.where(low_lane, upper, swap(lower)) if side == 0 else jnp.where(low_lane, swap(upper), lower)

    def mine_spectra(p):
        def step(i, _):
            at = pl.multiple_of(i * N, N)
            if p == 0:
                blocks = [own[pl.ds(at, N), j * N : j * N + N] for j in range(SIDE)]
            else:
                at = pl.multiple_of(at + HALF, HALF)
                blocks = [ext[0, pl.ds(at, N), j * N + N : j * N + 2 * N] for j in range(SIDE)]
            found = forward(jnp.concatenate(blocks, 0), t)
            for j in range(SIDE):
                spec[9 * p + SIDE * i + j] = found[j * N : j * N + N]
            return 0

        lax.fori_loop(0, SIDE, step, 0)

    mine_spectra(0)

    pl.semaphore_wait(barrier, expected)

    def remote(src, dst, send, recv, target):
        return pltpu.make_async_remote_copy(
            src_ref=src, dst_ref=dst, send_sem=send, recv_sem=recv, device_id=target, device_id_type=MESH
        )

    def col_rim(p, side):
        e = 2 * side - 1
        return remote(
            packed.at[1 - p, side], landed.at[p, 1 - side], cs.at[2 * p + side], cr.at[2 * p + 1 - side], there(-p, 0, e)
        )

    def tile_copy():
        return remote(images.at[0], ext.at[1, HALF : HALF + TILE, N : N + TILE], ts.at[0], tr.at[0], there(-1, 0, 0))

    turn_y = 2 * half - 1
    has_cross = (y + turn_y >= 0) & (y + turn_y < ny_)
    first_at, last_at = 0, HALF + TILE

    def takes(at_y):
        return ny_ - 1 - at_y

    def rows_of(kind):
        return HALF // PARTS[kind]

    def rim_at(kind, of_half):
        return of_half * last_at if kind else (1 - of_half) * last_at

    def leg(p, kind, k, m):
        sign = 1 - 2 * p
        n = rows_of(kind)
        index = ((p * 2 + kind) * LEGS + k) * PARTS[1] + m
        if k == 0:
            top = pl.multiple_of((half if kind else 1 - half) * (TILE - HALF) + m * n, 8)
            src = images.at[1 - p, pl.ds(top, n), :]
            to_y = y
            if kind:
                early = ((half == 1) & (m >= takes(y))) | ((half == 0) & (m < takes(y - 1)))
                to_y = jnp.where(early, y + turn_y, y)
            target = on_line(-p, to_y, z + sign * hop)
        else:
            src = transit.at[p, kind, k - 1, pl.ds(m * n, n), :]
            to_y = y
            if kind and k == LEGS - 1:
                from_half = half_at(z - sign * hop * k)
                late = ((from_half == 1) & (m < takes(y))) | ((from_half == 0) & (m > takes(y)))
                to_y = jnp.where(late, y + 2 * from_half - 1, y)
            target = on_line(0, to_y, z + sign * hop)
        if k == LEGS - 1:
            at = pl.multiple_of(rim_at(kind, half_at(z + sign * hop)) + m * n, 8)
            dst = ext.at[p, pl.ds(at, n), N : N + TILE]
        else:
            dst = transit.at[p, kind, k, pl.ds(m * n, n), :]
        return remote(src, dst, rs.at[index], rr.at[index], target)

    def leg_comes(p, kind, k, m):
        ok = s + p < ns_
        if kind:
            ok = ok & (has_cross if k == LEGS - 1 else m != takes(y))
        return ok

    def leg_goes(p, kind, k, m):
        if k:
            return leg_comes(p, kind, k - 1, m)
        return (s - p >= 0) & has_cross if kind else s - p >= 0

    def begin(kind, pairs=(0, 1)):
        for m in range(PARTS[kind]):
            for p in pairs:
                @pl.when(leg_goes(p, kind, 0, m))
                def _(p=p, m=m):
                    leg(p, kind, 0, m).start()

    def pass_on(kind, k):
        for m in range(PARTS[kind]):
            for p in range(2):
                @pl.when(leg_comes(p, kind, k, m))
                def _(p=p, m=m):
                    leg(p, kind, k, m).wait_recv()
                    if k < LEGS - 1:
                        leg(p, kind, k + 1, m).start()

    def corner(p, kind, side):
        at = pl.multiple_of(rim_at(kind, half), 8)
        src = slice(TILE, TILE + N) if side else slice(N, 2 * N)
        dst = slice(0, N) if side else slice(N + TILE, 2 * N + TILE)
        n = 4 * p + 2 * kind
        rows = pl.ds(at, HALF)
        return remote(
            ext.at[p, rows, src], ext.at[p, rows, dst], ks.at[n + side], kr.at[n + 1 - side], there(0, 0, 2 * side - 1)
        )

    def corner_moves(p, kind, e):
        ok = (s + p < ns_) & inside(0, 0, e)
        return ok & has_cross if kind else ok

    def send_corners(kind):
        for p in range(2):
            for side in range(2):
                @pl.when(corner_moves(p, kind, 2 * side - 1))
                def _(p=p, side=side):
                    corner(p, kind, side).start()

    def await_corners(kind, p):
        for side in range(2):
            @pl.when(corner_moves(p, kind, 1 - 2 * side))
            def _(side=side):
                corner(p, kind, side).wait_recv()

    def frame_copy(b, e):
        n, m = 3 * (b + 1) + e + 1, 3 * (1 - b) + 1 - e
        return remote(ftile, fslots.at[m], fs.at[n], fr.at[m], there(0, b, e))

    def match(vertices):
        lane = iota((N, N), 1)
        row = iota((N, N), 0)
        low = lane < HALF
        found = dtile[...]
        stack = []
        for p, i, j in vertices:
            top = i * N

            def at(first, rows, block):
                if not isinstance(i, int):
                    first = pl.multiple_of(first, HALF)
                return ext[p, pl.ds(first, rows), block * N : block * N + N]

            def beside(first, rows):
                left, right = at(first, rows, j), at(first, rows, j + 2)
                return jnp.where(low[:rows], right, left)

            dy, dx = off[0, i, p, j], off[1, i, p, j]
            in_rows = (row >= dy) & (row < dy + N)
            in_cols = (lane >= dx) & (lane < dx + N)
            main = jnp.where(in_cols, at(top + HALF, N, j + 1), beside(top + HALF, N))
            over = jnp.concatenate([at(top + HALF + N, HALF, j + 1), at(top, HALF, j + 1)], 0)
            over_side = jnp.concatenate([beside(top + HALF + N, HALF), beside(top, HALF)], 0)
            stack.append(jnp.where(in_rows, main, jnp.where(in_cols, over, over_side)))
        theirs = forward(jnp.concatenate(stack, 0), t)
        scores = inverse(
            jnp.concatenate(
                [cross(spec[9 * p + SIDE * i + j], theirs[k * N : k * N + N]) for k, (p, i, j) in enumerate(vertices)], 0
            ),
            t,
        )
        shifts = [(off[0, i, p, j], off[1, i, p, j]) for p, i, j in vertices]
        for comp, found_shifts in enumerate(peaks(scores, shifts)):
            for k, (p, i, j) in enumerate(vertices):
                value = (shifts[k][comp].astype(F32) + found_shifts[k : k + 1]) * (1.0 / N)
                found = jnp.where((row8 == i) & (lane8 == 16 * (2 * comp + p) + j), value, found)
        dtile[...] = found

    def match_row(p, i):
        match([(p, i, j) for j in range(SIDE)])

    def fill_columns(p):
        for side in range(2):
            @pl.when(inside(p, 0, 1 - 2 * side))
            def _(side=side):
                col_rim(p, side).wait_recv()
        for side in range(2):
            got = landed[p, side]
            column = slice(0, N) if side == 0 else slice(N + TILE, 2 * N + TILE)
            turned = swap(got)
            upper, lower = (turned, got) if side == 0 else (got, turned)
            ext[p, HALF : HALF + TILE // 2, column] = upper
            ext[p, HALF + TILE // 2 : HALF + TILE, column] = lower

    dtile[...] = blank

    begin(0)
    for p in (0, 1):
        for side in range(2):
            @pl.when(inside(-p, 0, 2 * side - 1))
            def _(p=p, side=side):
                col_rim(p, side).start()
    begin(1)

    @pl.when(s > 0)
    def _():
        tile_copy().start()

    mine_spectra(1)
    for k in range(LEGS - 1):
        pass_on(0, k)
        pass_on(1, k)
        if k == 0:
            fill_columns(0)
            match_row(0, 1)
        if k == min(1, LEGS - 2):
            @pl.when(s < ns_ - 1)
            def _():
                tile_copy().wait_recv()

            fill_columns(1)
            match_row(1, 1)
    pass_on(0, LEGS - 1)
    send_corners(0)
    along = 2 * (1 - half)
    for p in range(2):
        await_corners(0, p)
        match_row(p, along)
    pass_on(1, LEGS - 1)
    send_corners(1)
    across = 2 * half
    match([(p, across, 1) for p in range(2)])
    for p in range(2):
        await_corners(1, p)
    match([(p, across, j) for p in range(2) for j in (0, 2)])

    silent = (s == ns_ - 1) & ((lane8 & 16) != 0)
    found = jnp.where(silent, 0.0, dtile[...])
    dtile[...] = found

    def total_copy(k):
        return remote(dtile, dslots.at[s], ds.at[k], dr.at[s], (k, r, c))

    def total_arrival(k):
        return remote(dtile, dslots.at[k], ds.at[k], dr.at[k], (k, r, c))

    for k in range(ns_ - 1, 0, -1):
        @pl.when(k > s)
        def _(k=k):
            total_copy(k).start()
    for g in range(4):
        disp_ref[g // 2, :, g % 2] = (pltpu.roll(found, N - 16 * g, 1) if g else found)[0:SIDE, 0:SIDE]
    strips[...] = jnp.zeros_like(strips)

    for k in range(ns_ - 1):
        @pl.when(k < s)
        def _(k=k):
            total_arrival(k).wait_recv()
    lower = dslots[0]
    for k in range(1, ns_ - 1):
        lower = lower + dslots[k]
    second = (lane8 & 16) != 0
    below = lower + jnp.where(second, pltpu.roll(lower, 16, 1), pltpu.roll(lower, N - 16, 1))
    below = below + jnp.where(second, pltpu.roll(found, 16, 1), 0.0)
    ftile[...] = held + pltpu.roll(start - below, 4 * SIDE, 1)
    for b, e in near:
        @pl.when(inside(0, b, e))
        def _(b=b, e=e):
            frame_copy(b, e).start()

    for p in (0, 1):
        for side in range(2):
            @pl.when(inside(-p, 0, 2 * side - 1))
            def _(p=p, side=side):
                col_rim(p, side).wait_send()

            for kind in range(2):
                @pl.when(corner_moves(p, kind, 2 * side - 1))
                def _(p=p, kind=kind, side=side):
                    corner(p, kind, side).wait_send()

        for kind in range(2):
            for k in range(LEGS):
                for m in range(PARTS[kind]):
                    @pl.when(leg_goes(p, kind, k, m))
                    def _(p=p, kind=kind, k=k, m=m):
                        leg(p, kind, k, m).wait_send()

    @pl.when(s > 0)
    def _():
        tile_copy().wait_send()

    for k in range(1, ns_):
        @pl.when(k > s)
        def _(k=k):
            total_copy(k).wait_send()
    for b, e in near:
        @pl.when(inside(0, b, e))
        def _(b=b, e=e):
            frame_copy(b, e).wait_send()
            frame_copy(-b, -e).wait_recv()

    for b in (-1, 0, 1):
        for e in (-1, 0, 1):
            at = SIDE * (b + 1)
            tile = ftile[...] if (b, e) == (0, 0) else fslots[3 * (b + 1) + e + 1]
            strips[e + 1, at : at + SIDE, :] = tile[0:SIDE]
    lane16 = iota((16, N), 1) & 15

    def frame(q):
        out = jnp.zeros((16, N), F32)
        for e in (-1, 0, 1):
            at = SIDE * (e + 1)
            by = (at - SIDE * q) % N
            strip = strips[e + 1]
            strip = pltpu.roll(strip, by, 1) if by else strip
            out = jnp.where((lane16 >= at) & (lane16 < at + SIDE), strip, out)
        return out

    v, right, down, anchor, target = (frame(q) for q in range(5))
    right_left = pltpu.roll(right, 1, 1)
    down_upper = pltpu.roll(down, 1, 0)
    for _ in range(ITERS):
        v = (
            v
            + right * (pltpu.roll(v, N - 1, 1) - v)
            + right_left * (pltpu.roll(v, 1, 1) - v)
            + down * (pltpu.roll(v, 15, 0) - v)
            + down_upper * (pltpu.roll(v, 1, 0) - v)
            + anchor * (target - v)
        )
    v = pltpu.roll(v, 16 - SIDE, 0)
    for g in range(4):
        warped_ref[g // 2, :, g % 2] = pltpu.roll(v, (N - 16 * g - SIDE) % N, 1)[0:SIDE, 0:SIDE]


def per_device(sizes, images, offsets, warp, stiffness, valid):
    vmem = pl.BlockSpec(memory_space=pltpu.VMEM)
    anywhere = pl.BlockSpec(memory_space=pl.ANY)
    dma = pltpu.SemaphoreType.DMA
    out = jax.ShapeDtypeStruct((2, SIDE, 2, SIDE), F32)
    n = sizes[0]
    turned = (0, 2, 1, 3)
    outs = pl.pallas_call(
        functools.partial(kernel, sizes),
        name="align",
        out_shape=(out, out),
        in_specs=[anywhere, pl.BlockSpec(memory_space=pltpu.SMEM), vmem, vmem, vmem, anywhere],
        out_specs=(vmem, vmem),
        scratch_shapes=[
            pltpu.VMEM((2 * N, 6 * N), BF),
            pltpu.VMEM((TILE, TILE), F32),
            pltpu.VMEM((2, TILE + 2 * HALF, TILE + 2 * N), F32),
            pltpu.VMEM((18, N, N), F32),
            pltpu.VMEM((2, 2, TILE // 2, N), F32),
            pltpu.VMEM((2, 2, TILE // 2, N), F32),
            pltpu.VMEM((2, 2, LEGS - 1, HALF, TILE), F32),
            pltpu.VMEM((10, 8, N), F32),
            pltpu.VMEM((8, N), F32),
            pltpu.VMEM((9, 8, N), F32),
            pltpu.VMEM((8, N), F32),
            pltpu.VMEM((n, 8, N), F32),
            pltpu.VMEM((3, 16, N), F32),
            dma((3,)),
            dma((1,)),
            dma((1,)),
            dma((4 * LEGS * PARTS[1],)),
            dma((4 * LEGS * PARTS[1],)),
            dma((4,)),
            dma((4,)),
            dma((8,)),
            dma((8,)),
            dma((n,)),
            dma((n,)),
            dma((9,)),
            dma((9,)),
        ],
        compiler_params=pltpu.CompilerParams(
            collective_id=0, has_side_effects=True, vmem_limit_bytes=60 * 1024 * 1024
        ),
    )(
        images,
        offsets.transpose(turned),
        warp.transpose(turned),
        stiffness.transpose(turned),
        valid.transpose(1, 0, 2),
        jnp.asarray(tables()),
    )
    return tuple(x.transpose(turned) for x in outs)


def solution(mesh):
    sizes = tuple(mesh.shape[a] for a in ("sec", "row", "col"))
    return jax.shard_map(
        functools.partial(per_device, sizes),
        mesh=mesh,
        in_specs=(
            P("sec", "row", "col"),
            P(None, "sec", "row", "col"),
            P(None, "sec", "row", "col"),
            P(None, "sec", "row", "col"),
            P("sec", "row", "col"),
        ),
        out_specs=(P(None, "sec", "row", "col"), P(None, "sec", "row", "col")),
        check_vma=False,
    )
```

```python
import functools

import jax
import jax.numpy as jnp
import ml_dtypes
import numpy as np
from jax import lax
from jax.experimental import pallas as pl
from jax.experimental.pallas import tpu as pltpu
from jax.sharding import PartitionSpec as P

MESH = pl.DeviceIdType.MESH
N = 128
HALF = 64
SIDE = 3
TILE = SIDE * N
BLOCKS = 2 * TILE // N
SHARPNESS = 80.0
ANCHOR = 0.2
ITERS = 3
LEGS = 4
PARTS = (2, 4)
BF = jnp.bfloat16
F32 = jnp.float32


def split3(a):
    high = a.astype(ml_dtypes.bfloat16)
    rest = a - high.astype(np.float64)
    mid = rest.astype(ml_dtypes.bfloat16)
    low = (rest - mid.astype(np.float64)).astype(ml_dtypes.bfloat16)
    return high, mid, low


def tables():
    x = np.arange(N)
    forward = np.zeros((N, N))
    for f in range(HALF):
        forward[f] = np.cos(2 * np.pi * ((f * x) % N) / N)
    forward[HALF] = 1 - 2 * (x % 2)
    for f in range(1, HALF):
        forward[HALF + f] = np.sin(2 * np.pi * ((f * x) % N) / N)
    scale = np.full(N, 2.0 / N)
    scale[0] = scale[HALF] = 1.0 / N
    inverse = (forward * scale[:, None]).T

    def right(a):
        h, m, l = split3(a)
        return np.block([[h, m], [h, m]]), np.concatenate([h, l], 0)

    return np.concatenate([*right(forward.T), *right(inverse.T * np.sqrt(SHARPNESS / (N * N)))], 1)


def parts(x):
    high = x.astype(BF)
    rest = x - high.astype(F32)
    mid = rest.astype(BF)
    low = (rest - mid.astype(F32)).astype(BF)
    return high, mid, low


def dot(a, b):
    return jnp.dot(a, b, preferred_element_type=F32)


def right_mul(x, wa, wb):
    high, mid, low = parts(x)
    a = dot(jnp.concatenate([high, mid], 1), wa)
    return a[:, :N] + a[:, N:] + dot(jnp.concatenate([low, high], 1), wb)


def turn(x):
    return jnp.concatenate([x[k : k + N].T for k in range(0, x.shape[0], N)], 0)


def forward(x, t):
    return right_mul(turn(right_mul(x, t[:, 0 : 2 * N], t[:, 2 * N : 3 * N])), t[:, 0 : 2 * N], t[:, 2 * N : 3 * N])


def inverse(x, t):
    return right_mul(turn(right_mul(x, t[:, 3 * N : 5 * N], t[:, 5 * N :])), t[:, 3 * N : 5 * N], t[:, 5 * N :])


def iota(shape, dim):
    return lax.broadcasted_iota(jnp.int32, shape, dim)


def swap(x):
    return pltpu.roll(x, HALF, 1)


def cross(mine, theirs):
    lane = iota((N, N), 1)
    single = (lane & (HALF - 1)) == 0
    turned = swap(theirs)
    first = jnp.where(single | (lane < HALF), theirs, -turned)
    second = jnp.where(single, 0.0, jnp.where(lane < HALF, turned, theirs))
    other = swap(mine)
    even, odd = slice(0, HALF), slice(HALF, N)

    def pair(a, b):
        return mine[a] * first[b] + other[a] * second[b]

    lone = iota((HALF, N), 0) == 0
    both = pair(odd, odd)
    top = pair(even, even) + jnp.where(lone, 0.0, both)
    top = jnp.where(lone & (iota((HALF, N), 1) == 0), 0.0, top)
    low = jnp.where(lone, both, pair(even, odd) - pair(odd, even))
    return jnp.concatenate([top, low], 0)


def peaks(scores, shifts):
    count = len(shifts)
    blocks = [scores[k * N : k * N + N] for k in range(count)]
    highest = jnp.concatenate([jnp.max(x, axis=0, keepdims=True) for x in blocks], 0)
    highest = jnp.max(highest, axis=1, keepdims=True)
    sums = []
    for k, (dy, dx) in enumerate(shifts):
        rows = (((iota((N, N), 0) - dy + HALF) & (N - 1)) - HALF).astype(F32)
        cols = (((iota((1, N), 1) - dx + HALF) & (N - 1)) - HALF).astype(F32)
        weights = jnp.exp(blocks[k] - highest[k : k + 1])
        by_col = jnp.sum(weights, axis=0, keepdims=True)
        sums.append((by_col, jnp.sum(weights * rows, axis=0, keepdims=True), by_col * cols))
    sums = [jnp.sum(jnp.concatenate([x[q] for x in sums], 0), axis=1, keepdims=True) for q in range(3)]
    return sums[1] / sums[0], sums[2] / sums[0]


def kernel(sizes, images, off_in, warp_in, stiff_in, valid_in, table, out_ref, *rest):
    (off, warp, stiff, valid, t, own, ext, spec, packed, landed, transit, cpacked, clanded) = rest[:13]
    (small, ftile, fslots, dtile, dslots, strips) = rest[13:19]
    lsem, ts, tr, rs, rr, cs, cr, ks, kr, ds, dr, fs, fr = rest[19:]
    ns_, nr_, nc_ = sizes
    ny_, nz_ = nr_ // 2, 2 * nc_
    hop = nc_ // LEGS
    s, r, c = lax.axis_index("sec"), lax.axis_index("row"), lax.axis_index("col")
    y, half = r // 2, lax.rem(r, 2)
    z = half * nc_ + c

    def inside(a, b, e):
        ok = None
        for at, by, n in ((s, a, ns_), (r, b, nr_), (c, e, nc_)):
            if by:
                here = (at + by >= 0) & (at + by < n)
                ok = here if ok is None else ok & here
        return ok

    def there(a, b, e):
        return (s + a, r + b, c + e)

    def on_line(a, to_y, to_z):
        to_z = lax.rem(to_z + 2 * nz_, nz_)
        return (s + a, 2 * to_y + to_z // nc_, lax.rem(to_z, nc_))

    def half_at(at_z):
        return lax.rem(at_z + 2 * nz_, nz_) // nc_

    barrier = pltpu.get_barrier_semaphore()
    goes = [(k, 0, 0) for k in range(1, ns_)] + [(-1, 0, 0), (-1, 0, -1), (-1, 0, 1), (0, 0, -1), (0, 0, 1)]
    expected = 0
    for a, b, e in goes:
        @pl.when(inside(-a, -b, -e))
        def _(a=a, b=b, e=e):
            pl.semaphore_signal(barrier, inc=1, device_id=there(-a, -b, -e), device_id_type=MESH)

        expected = expected + inside(a, b, e).astype(jnp.int32)
    for a, e in ((0, hop), (0, -hop), (-1, -hop)):
        for b in (-1, 0, 1):
            def both(sign, a=a, b=b):
                return (s + sign * a >= 0) & (s + sign * a < ns_) & (y + sign * b >= 0) & (y + sign * b < ny_)

            @pl.when(both(-1))
            def _(a=a, b=b, e=e):
                pl.semaphore_signal(barrier, inc=1, device_id=on_line(-a, y - b, z - e), device_id_type=MESH)

            expected = expected + both(1).astype(jnp.int32)

    locals_ = [
        pltpu.make_async_copy(src, dst, lsem.at[k])
        for k, (src, dst) in enumerate(
            (
                (images.at[1], ext.at[0, HALF : HALF + TILE, N : N + TILE]),
                (images.at[0], own),
                (table, t),
                (off_in, off),
                (warp_in, warp),
                (stiff_in, stiff),
                (valid_in, valid),
            )
        )
    ]
    for copy in locals_:
        copy.start()

    @pl.when(r == 0)
    def _():
        for p in range(2):
            ext[p, 0:HALF, :] = jnp.zeros((HALF, TILE + 2 * N), F32)

    @pl.when(r == nr_ - 1)
    def _():
        for p in range(2):
            ext[p, HALF + TILE :, :] = jnp.zeros((HALF, TILE + 2 * N), F32)

    @pl.when(c == 0)
    def _():
        for p in range(2):
            ext[p, 0:HALF, 0:N] = jnp.zeros((HALF, N), F32)
            ext[p, HALF + TILE :, 0:N] = jnp.zeros((HALF, N), F32)
            landed[p, 0] = jnp.zeros((TILE // 2, N), F32)

    @pl.when(c == nc_ - 1)
    def _():
        for p in range(2):
            ext[p, 0:HALF, N + TILE :] = jnp.zeros((HALF, N), F32)
            ext[p, HALF + TILE :, N + TILE :] = jnp.zeros((HALF, N), F32)
            landed[p, 1] = jnp.zeros((TILE // 2, N), F32)

    @pl.when(s == ns_ - 1)
    def _():
        ext[1] = jnp.zeros((TILE + 2 * HALF, TILE + 2 * N), F32)
        landed[1] = jnp.zeros((2, TILE // 2, N), F32)

    near = [(b, e) for b in (-1, 0, 1) for e in (-1, 0, 1) if (b, e) != (0, 0)]
    blank = jnp.zeros((8, N), F32)
    for b, e in near:
        @pl.when(jnp.logical_not(inside(0, b, e)))
        def _(b=b, e=e):
            fslots[3 * (b + 1) + e + 1] = blank

    for k in range(ns_):
        @pl.when(s <= k)
        def _(k=k):
            dslots[k] = blank

    for copy in locals_[:2]:
        copy.wait()

    def pack(strip, side):
        count = strip.shape[0] // 2
        upper, lower = strip[:count], strip[count:]
        low = iota((count, N), 1) < HALF
        return jnp.where(low, swap(upper), lower) if side else jnp.where(low, upper, swap(lower))

    def unpack(got, side):
        turned = swap(got)
        return (got, turned) if side else (turned, got)

    for im in range(2):
        for side in range(2):
            if im == 0:
                strip = own[:, 0:N] if side == 0 else own[:, TILE - N :]
            else:
                strip = ext[0, HALF : HALF + TILE, N : 2 * N] if side == 0 else ext[0, HALF : HALF + TILE, TILE : TILE + N]
            packed[im, side] = pack(strip, side)

    def mine_spectra(p):
        def step(i, _):
            at = pl.multiple_of(i * N, N)
            if p == 0:
                blocks = [own[pl.ds(at, N), j * N : j * N + N] for j in range(SIDE)]
            else:
                at = pl.multiple_of(at + HALF, HALF)
                blocks = [ext[0, pl.ds(at, N), j * N + N : j * N + 2 * N] for j in range(SIDE)]
            found = forward(jnp.concatenate(blocks, 0), t)
            for j in range(SIDE):
                spec[9 * p + SIDE * i + j] = found[j * N : j * N + N]
            return 0

        lax.fori_loop(0, SIDE, step, 0)

    pl.semaphore_wait(barrier, expected)

    def remote(src, dst, send, recv, target):
        return pltpu.make_async_remote_copy(
            src_ref=src, dst_ref=dst, send_sem=send, recv_sem=recv, device_id=target, device_id_type=MESH
        )

    def col_rim(p, side):
        e = 2 * side - 1
        return remote(
            packed.at[1 - p, side], landed.at[p, 1 - side], cs.at[2 * p + side], cr.at[2 * p + 1 - side], there(-p, 0, e)
        )

    def tile_copy():
        return remote(images.at[0], ext.at[1, HALF : HALF + TILE, N : N + TILE], ts.at[0], tr.at[0], there(-1, 0, 0))

    turn_y = 2 * half - 1
    has_cross = (y + turn_y >= 0) & (y + turn_y < ny_)
    first_at, last_at = 0, HALF + TILE

    def takes(at_y):
        return ny_ - 1 - at_y

    def rows_of(kind):
        return HALF // PARTS[kind]

    def rim_at(kind, of_half):
        return of_half * last_at if kind else (1 - of_half) * last_at

    def leg(p, kind, k, m, block=None):
        sign = 1 - 2 * p
        n = rows_of(kind)
        index = (p * 2 + kind) * PARTS[1] + m
        index = index * (LEGS - 1) + k if block is None else 4 * PARTS[1] * (LEGS - 1) + index * SIDE + block
        lanes = slice(0, TILE) if block is None else slice(block * N, block * N + N)
        if k == 0:
            top = pl.multiple_of((half if kind else 1 - half) * (TILE - HALF) + m * n, 8)
            src = images.at[1 - p, pl.ds(top, n), :]
            to_y = y
            if kind:
                early = ((half == 1) & (m >= takes(y))) | ((half == 0) & (m < takes(y - 1)))
                to_y = jnp.where(early, y + turn_y, y)
            target = on_line(-p, to_y, z + sign * hop)
        else:
            src = transit.at[p, kind, k - 1, pl.ds(m * n, n), lanes]
            to_y = y
            if kind and k == LEGS - 1:
                from_half = half_at(z - sign * hop * k)
                late = ((from_half == 1) & (m < takes(y))) | ((from_half == 0) & (m > takes(y)))
                to_y = jnp.where(late, y + 2 * from_half - 1, y)
            target = on_line(0, to_y, z + sign * hop)
        if k == LEGS - 1:
            at = pl.multiple_of(rim_at(kind, half_at(z + sign * hop)) + m * n, 8)
            dst = ext.at[p, pl.ds(at, n), lanes.start + N : lanes.stop + N]
        else:
            dst = transit.at[p, kind, k, pl.ds(m * n, n), :]
        return remote(src, dst, rs.at[index], rr.at[index], target)

    def leg_comes(p, kind, k, m):
        ok = s + p < ns_
        if kind:
            ok = ok & (has_cross if k == LEGS - 1 else m != takes(y))
        return ok

    def leg_goes(p, kind, k, m):
        if k:
            return leg_comes(p, kind, k - 1, m)
        return (s - p >= 0) & has_cross if kind else s - p >= 0

    def begin(kind, pairs=(0, 1)):
        for m in range(PARTS[kind]):
            for p in pairs:
                @pl.when(leg_goes(p, kind, 0, m))
                def _(p=p, m=m):
                    leg(p, kind, 0, m).start()

    def each_part(kind, condition, k, act):
        for m in range(PARTS[kind]):
            for p in range(2):
                @pl.when(condition(p, kind, k, m))
                def _(p=p, m=m):
                    act(p, m)

    def pass_on(kind, k):
        def act(p, m):
            leg(p, kind, k, m).wait_recv()
            if k < LEGS - 2:
                leg(p, kind, k + 1, m).start()
            else:
                leg(p, kind, k + 1, m, 0).start()
                leg(p, kind, k + 1, m, SIDE - 1).start()

        each_part(kind, leg_comes, k, act)
        if k == LEGS - 2:
            each_part(kind, leg_comes, k, lambda p, m: leg(p, kind, k + 1, m, 1).start())

    def arrive(kind, blocks):
        def act(p, m):
            for block in blocks:
                leg(p, kind, LEGS - 1, m, block).wait_recv()

        each_part(kind, leg_comes, LEGS - 1, act)

    def corner(p, kind, side):
        n = 4 * p + 2 * kind
        return remote(
            cpacked.at[p, kind, side],
            clanded.at[p, kind, 1 - side],
            ks.at[n + side],
            kr.at[n + 1 - side],
            there(0, 0, 2 * side - 1),
        )

    def rim_rows(kind):
        return pl.ds(pl.multiple_of(rim_at(kind, half), HALF), HALF)

    def corner_moves(p, kind, e):
        ok = (s + p < ns_) & inside(0, 0, e)
        return ok & has_cross if kind else ok

    def send_corners(kind):
        for p in range(2):
            for side in range(2):
                @pl.when(corner_moves(p, kind, 2 * side - 1))
                def _(p=p, side=side):
                    src = slice(TILE, TILE + N) if side else slice(N, 2 * N)
                    cpacked[p, kind, side] = pack(ext[p, rim_rows(kind), src], side)
                    corner(p, kind, side).start()

    def await_corners(kind, p):
        for side in range(2):
            @pl.when(corner_moves(p, kind, 1 - 2 * side))
            def _(side=side):
                corner(p, kind, side).wait_recv()
                dst = slice(0, N) if side else slice(N + TILE, 2 * N + TILE)
                ext[p, rim_rows(kind), dst] = jnp.concatenate(unpack(clanded[p, kind, 1 - side], 1 - side), 0)

    def frame_copy(b, e):
        n, m = 3 * (b + 1) + e + 1, 3 * (1 - b) + 1 - e
        return remote(ftile, fslots.at[m], fs.at[n], fr.at[m], there(0, b, e))

    def match(vertices):
        lane = iota((N, N), 1)
        row = iota((N, N), 0)
        low = lane < HALF
        found = dtile[...]
        stack = []
        for p, i, j in vertices:
            top = i * N

            def at(first, rows, block):
                if not isinstance(i, int):
                    first = pl.multiple_of(first, HALF)
                return ext[p, pl.ds(first, rows), block * N : block * N + N]

            def beside(first, rows):
                left, right = at(first, rows, j), at(first, rows, j + 2)
                return jnp.where(low[:rows], right, left)

            dy, dx = off[0, i, p, j], off[1, i, p, j]
            in_rows = (row >= dy) & (row < dy + N)
            in_cols = (lane >= dx) & (lane < dx + N)
            main = jnp.where(in_cols, at(top + HALF, N, j + 1), beside(top + HALF, N))
            over = jnp.concatenate([at(top + HALF + N, HALF, j + 1), at(top, HALF, j + 1)], 0)
            over_side = jnp.concatenate([beside(top + HALF + N, HALF), beside(top, HALF)], 0)
            stack.append(jnp.where(in_rows, main, jnp.where(in_cols, over, over_side)))
        theirs = forward(jnp.concatenate(stack, 0), t)
        scores = inverse(
            jnp.concatenate(
                [cross(spec[9 * p + SIDE * i + j], theirs[k * N : k * N + N]) for k, (p, i, j) in enumerate(vertices)], 0
            ),
            t,
        )
        shifts = [(off[0, i, p, j], off[1, i, p, j]) for p, i, j in vertices]
        for comp, found_shifts in enumerate(peaks(scores, shifts)):
            for k, (p, i, j) in enumerate(vertices):
                value = (shifts[k][comp].astype(F32) + found_shifts[k : k + 1]) * (1.0 / N)
                found = jnp.where((row8 == i) & (lane8 == 16 * (2 * comp + p) + j), value, found)
        dtile[...] = found

    def match_row(p, i):
        match([(p, i, j) for j in range(SIDE)])

    def fill_columns(p):
        for side in range(2):
            @pl.when(inside(p, 0, 1 - 2 * side))
            def _(side=side):
                col_rim(p, side).wait_recv()
        for side in range(2):
            column = slice(0, N) if side == 0 else slice(N + TILE, 2 * N + TILE)
            upper, lower = unpack(landed[p, side], side)
            ext[p, HALF : HALF + TILE // 2, column] = upper
            ext[p, HALF + TILE // 2 : HALF + TILE, column] = lower

    begin(0)
    for p in (0, 1):
        for side in range(2):
            @pl.when(inside(-p, 0, 2 * side - 1))
            def _(p=p, side=side):
                col_rim(p, side).start()
    begin(1)

    @pl.when(s > 0)
    def _():
        tile_copy().start()

    for copy in locals_[2:]:
        copy.wait()
    mine_spectra(0)
    pass_on(0, 0)
    pass_on(1, 0)
    row8, lane8 = iota((8, N), 0), iota((8, N), 1)
    small[...] = jnp.zeros_like(small)
    for comp in range(2):
        for sec in range(2):
            small[2 * comp + sec, 0:SIDE, 0:SIDE] = warp[comp, :, sec]
            small[4 + 2 * comp + sec, 0:SIDE, 0:SIDE] = stiff[comp, :, sec]
    for sec in range(2):
        small[8 + sec, 0:SIDE, 0:SIDE] = ANCHOR * valid[:, sec].astype(F32)
    dtile[...] = blank
    start = jnp.zeros((8, N), F32)
    held = jnp.zeros((8, N), F32)
    for g in range(4):
        sec = g % 2
        w = small[g]
        right = jnp.where((c == nc_ - 1) & (lane8 == SIDE - 1), 0.0, small[4 + sec])
        down = jnp.where((r == nr_ - 1) & (row8 == SIDE - 1), 0.0, small[6 + sec])
        start = start + (pltpu.roll(w, 16 * g, 1) if g else w)
        for q, quantity in enumerate((w, right, down, small[8 + sec])):
            by = 16 * g + SIDE * q
            held = held + (pltpu.roll(quantity, by, 1) if by else quantity)

    mine_spectra(1)
    fill_columns(0)
    for k in range(1, LEGS - 1):
        pass_on(0, k)
        pass_on(1, k)
        if k == 1:
            match_row(0, 1)
    if LEGS < 3:
        match_row(0, 1)

    @pl.when(s < ns_ - 1)
    def _():
        tile_copy().wait_recv()

    fill_columns(1)
    match_row(1, 1)
    along, across = 2 * (1 - half), 2 * half
    arrive(0, (0, SIDE - 1))
    send_corners(0)
    arrive(0, (1,))
    match([(p, along, 1) for p in range(2)])
    arrive(1, (0, SIDE - 1))
    send_corners(1)
    arrive(1, (1,))
    match([(p, across, 1) for p in range(2)])
    for kind, i in ((0, along), (1, across)):
        for p in range(2):
            await_corners(kind, p)
        match([(p, i, j) for p in range(2) for j in (0, 2)])

    silent = (s == ns_ - 1) & ((lane8 & 16) != 0)
    found = jnp.where(silent, 0.0, dtile[...])
    dtile[...] = found

    def total_copy(k):
        return remote(dtile, dslots.at[s], ds.at[k], dr.at[s], (k, r, c))

    def total_arrival(k):
        return remote(dtile, dslots.at[k], ds.at[k], dr.at[k], (k, r, c))

    for k in range(ns_ - 1, 0, -1):
        @pl.when(k > s)
        def _(k=k):
            total_copy(k).start()
    for g in range(4):
        out_ref[0, g // 2, :, g % 2] = (pltpu.roll(found, N - 16 * g, 1) if g else found)[0:SIDE, 0:SIDE]
    strips[...] = jnp.zeros_like(strips)

    for k in range(ns_ - 1):
        @pl.when(k < s)
        def _(k=k):
            total_arrival(k).wait_recv()
    lower = dslots[0]
    for k in range(1, ns_ - 1):
        lower = lower + dslots[k]
    second = (lane8 & 16) != 0
    below = lower + jnp.where(second, pltpu.roll(lower, 16, 1), pltpu.roll(lower, N - 16, 1))
    below = below + jnp.where(second, pltpu.roll(found, 16, 1), 0.0)
    ftile[...] = held + pltpu.roll(start - below, 4 * SIDE, 1)
    for b, e in near:
        @pl.when(inside(0, b, e))
        def _(b=b, e=e):
            frame_copy(b, e).start()

    for p in (0, 1):
        for side in range(2):
            @pl.when(inside(-p, 0, 2 * side - 1))
            def _(p=p, side=side):
                col_rim(p, side).wait_send()

            for kind in range(2):
                @pl.when(corner_moves(p, kind, 2 * side - 1))
                def _(p=p, kind=kind, side=side):
                    corner(p, kind, side).wait_send()

        for kind in range(2):
            for k in range(LEGS):
                for m in range(PARTS[kind]):
                    @pl.when(leg_goes(p, kind, k, m))
                    def _(p=p, kind=kind, k=k, m=m):
                        for block in range(SIDE) if k == LEGS - 1 else (None,):
                            leg(p, kind, k, m, block).wait_send()

    @pl.when(s > 0)
    def _():
        tile_copy().wait_send()

    for k in range(1, ns_):
        @pl.when(k > s)
        def _(k=k):
            total_copy(k).wait_send()
    for b, e in near:
        @pl.when(inside(0, b, e))
        def _(b=b, e=e):
            frame_copy(b, e).wait_send()
            frame_copy(-b, -e).wait_recv()

    for b in (-1, 0, 1):
        for e in (-1, 0, 1):
            at = SIDE * (b + 1)
            tile = ftile[...] if (b, e) == (0, 0) else fslots[3 * (b + 1) + e + 1]
            strips[e + 1, at : at + SIDE, :] = tile[0:SIDE]
    lane16 = iota((16, N), 1) & 15

    def frame(q):
        out = jnp.zeros((16, N), F32)
        for e in (-1, 0, 1):
            at = SIDE * (e + 1)
            by = (at - SIDE * q) % N
            strip = strips[e + 1]
            strip = pltpu.roll(strip, by, 1) if by else strip
            out = jnp.where((lane16 >= at) & (lane16 < at + SIDE), strip, out)
        return out

    v, right, down, anchor, target = (frame(q) for q in range(5))
    right_left = pltpu.roll(right, 1, 1)
    down_upper = pltpu.roll(down, 1, 0)
    for _ in range(ITERS):
        v = (
            v
            + right * (pltpu.roll(v, N - 1, 1) - v)
            + right_left * (pltpu.roll(v, 1, 1) - v)
            + down * (pltpu.roll(v, 15, 0) - v)
            + down_upper * (pltpu.roll(v, 1, 0) - v)
            + anchor * (target - v)
        )
    v = pltpu.roll(v, 16 - SIDE, 0)
    for g in range(4):
        out_ref[1, g // 2, :, g % 2] = pltpu.roll(v, (N - 16 * g - SIDE) % N, 1)[0:SIDE, 0:SIDE]


def per_device(sizes, images, offsets, warp, stiffness, valid):
    vmem = pl.BlockSpec(memory_space=pltpu.VMEM)
    anywhere = pl.BlockSpec(memory_space=pl.ANY)
    dma = pltpu.SemaphoreType.DMA
    out = jax.ShapeDtypeStruct((2, 2, SIDE, 2, SIDE), F32)
    n = sizes[0]
    turned = (0, 2, 1, 3)
    outs = pl.pallas_call(
        functools.partial(kernel, sizes),
        name="align",
        out_shape=out,
        in_specs=[anywhere] * 6,
        out_specs=vmem,
        scratch_shapes=[
            pltpu.SMEM((2, SIDE, 2, SIDE), jnp.int32),
            pltpu.VMEM((2, SIDE, 2, SIDE), F32),
            pltpu.VMEM((2, SIDE, 2, SIDE), F32),
            pltpu.VMEM((SIDE, 2, SIDE), jnp.int32),
            pltpu.VMEM((2 * N, 6 * N), BF),
            pltpu.VMEM((TILE, TILE), F32),
            pltpu.VMEM((2, TILE + 2 * HALF, TILE + 2 * N), F32),
            pltpu.VMEM((18, N, N), F32),
            pltpu.VMEM((2, 2, TILE // 2, N), F32),
            pltpu.VMEM((2, 2, TILE // 2, N), F32),
            pltpu.VMEM((2, 2, LEGS - 1, HALF, TILE), F32),
            pltpu.VMEM((2, 2, 2, HALF // 2, N), F32),
            pltpu.VMEM((2, 2, 2, HALF // 2, N), F32),
            pltpu.VMEM((10, 8, N), F32),
            pltpu.VMEM((8, N), F32),
            pltpu.VMEM((9, 8, N), F32),
            pltpu.VMEM((8, N), F32),
            pltpu.VMEM((n, 8, N), F32),
            pltpu.VMEM((3, 16, N), F32),
            dma((7,)),
            dma((1,)),
            dma((1,)),
            dma((4 * PARTS[1] * (LEGS + 2),)),
            dma((4 * PARTS[1] * (LEGS + 2),)),
            dma((4,)),
            dma((4,)),
            dma((8,)),
            dma((8,)),
            dma((n,)),
            dma((n,)),
            dma((9,)),
            dma((9,)),
        ],
        compiler_params=pltpu.CompilerParams(
            collective_id=0, has_side_effects=True, vmem_limit_bytes=60 * 1024 * 1024
        ),
    )(
        images,
        offsets.transpose(turned),
        warp.transpose(turned),
        stiffness.transpose(turned),
        valid.transpose(1, 0, 2),
        jnp.asarray(tables()),
    )
    return tuple(x.transpose(turned) for x in outs)


def solution(mesh):
    sizes = tuple(mesh.shape[a] for a in ("sec", "row", "col"))
    return jax.shard_map(
        functools.partial(per_device, sizes),
        mesh=mesh,
        in_specs=(
            P("sec", "row", "col"),
            P(None, "sec", "row", "col"),
            P(None, "sec", "row", "col"),
            P(None, "sec", "row", "col"),
            P("sec", "row", "col"),
        ),
        out_specs=(P(None, "sec", "row", "col"), P(None, "sec", "row", "col")),
        check_vma=False,
    )
```

```python
import functools

import jax
import jax.numpy as jnp
import ml_dtypes
import numpy as np
from jax import lax
from jax.experimental import pallas as pl
from jax.experimental.pallas import tpu as pltpu
from jax.sharding import PartitionSpec as P

MESH = pl.DeviceIdType.MESH
N = 128
HALF = 64
SIDE = 3
TILE = SIDE * N
BLOCKS = 2 * TILE // N
SHARPNESS = 80.0
ANCHOR = 0.2
ITERS = 3
LEGS = 4
PARTS = (4, 4)
BF = jnp.bfloat16
F32 = jnp.float32


def split3(a):
    high = a.astype(ml_dtypes.bfloat16)
    rest = a - high.astype(np.float64)
    mid = rest.astype(ml_dtypes.bfloat16)
    low = (rest - mid.astype(np.float64)).astype(ml_dtypes.bfloat16)
    return high, mid, low


def tables():
    x = np.arange(N)
    forward = np.zeros((N, N))
    for f in range(HALF):
        forward[f] = np.cos(2 * np.pi * ((f * x) % N) / N)
    forward[HALF] = 1 - 2 * (x % 2)
    for f in range(1, HALF):
        forward[HALF + f] = np.sin(2 * np.pi * ((f * x) % N) / N)
    scale = np.full(N, 2.0 / N)
    scale[0] = scale[HALF] = 1.0 / N
    inverse = (forward * scale[:, None]).T

    def right(a):
        h, m, l = split3(a)
        return np.block([[h, m], [h, m]]), np.concatenate([h, l], 0)

    return np.concatenate([*right(forward.T), *right(inverse.T * np.sqrt(SHARPNESS / (N * N)))], 1)


def parts(x):
    high = x.astype(BF)
    rest = x - high.astype(F32)
    mid = rest.astype(BF)
    low = (rest - mid.astype(F32)).astype(BF)
    return high, mid, low


def dot(a, b):
    return jnp.dot(a, b, preferred_element_type=F32)


def right_mul(x, wa, wb):
    high, mid, low = parts(x)
    a = dot(jnp.concatenate([high, mid], 1), wa)
    return a[:, :N] + a[:, N:] + dot(jnp.concatenate([low, high], 1), wb)


def turn(x):
    return jnp.concatenate([x[k : k + N].T for k in range(0, x.shape[0], N)], 0)


def forward(x, t):
    return right_mul(turn(right_mul(x, t[:, 0 : 2 * N], t[:, 2 * N : 3 * N])), t[:, 0 : 2 * N], t[:, 2 * N : 3 * N])


def inverse(x, t):
    return right_mul(turn(right_mul(x, t[:, 3 * N : 5 * N], t[:, 5 * N :])), t[:, 3 * N : 5 * N], t[:, 5 * N :])


def iota(shape, dim):
    return lax.broadcasted_iota(jnp.int32, shape, dim)


def swap(x):
    return pltpu.roll(x, HALF, 1)


def cross(mine, theirs):
    lane = iota((N, N), 1)
    single = (lane & (HALF - 1)) == 0
    turned = swap(theirs)
    first = jnp.where(single | (lane < HALF), theirs, -turned)
    second = jnp.where(single, 0.0, jnp.where(lane < HALF, turned, theirs))
    other = swap(mine)
    even, odd = slice(0, HALF), slice(HALF, N)

    def pair(a, b):
        return mine[a] * first[b] + other[a] * second[b]

    lone = iota((HALF, N), 0) == 0
    both = pair(odd, odd)
    top = pair(even, even) + jnp.where(lone, 0.0, both)
    top = jnp.where(lone & (iota((HALF, N), 1) == 0), 0.0, top)
    low = jnp.where(lone, both, pair(even, odd) - pair(odd, even))
    return jnp.concatenate([top, low], 0)


def peaks(scores, shifts):
    count = len(shifts)
    blocks = [scores[k * N : k * N + N] for k in range(count)]
    highest = jnp.concatenate([jnp.max(x, axis=0, keepdims=True) for x in blocks], 0)
    highest = jnp.max(highest, axis=1, keepdims=True)
    sums = []
    for k, (dy, dx) in enumerate(shifts):
        rows = (((iota((N, N), 0) - dy + HALF) & (N - 1)) - HALF).astype(F32)
        cols = (((iota((1, N), 1) - dx + HALF) & (N - 1)) - HALF).astype(F32)
        weights = jnp.exp(blocks[k] - highest[k : k + 1])
        by_col = jnp.sum(weights, axis=0, keepdims=True)
        sums.append((by_col, jnp.sum(weights * rows, axis=0, keepdims=True), by_col * cols))
    sums = [jnp.sum(jnp.concatenate([x[q] for x in sums], 0), axis=1, keepdims=True) for q in range(3)]
    return sums[1] / sums[0], sums[2] / sums[0]


def kernel(sizes, images, off_in, warp_in, stiff_in, valid_in, table, out_ref, *rest):
    (off, warp, stiff, valid, t, own, ext, spec, packed, landed, transit, cpacked, clanded) = rest[:13]
    (small, ftile, fslots, dtile, dslots, strips) = rest[13:19]
    lsem, ts, tr, rs, rr, cs, cr, ks, kr, ds, dr, fs, fr = rest[19:]
    ns_, nr_, nc_ = sizes
    ny_, nz_ = nr_ // 2, 2 * nc_
    hop = nc_ // LEGS
    s, r, c = lax.axis_index("sec"), lax.axis_index("row"), lax.axis_index("col")
    y, half = r // 2, lax.rem(r, 2)
    z = half * nc_ + c

    def inside(a, b, e):
        ok = None
        for at, by, n in ((s, a, ns_), (r, b, nr_), (c, e, nc_)):
            if by:
                here = (at + by >= 0) & (at + by < n)
                ok = here if ok is None else ok & here
        return ok

    def there(a, b, e):
        return (s + a, r + b, c + e)

    def on_line(a, to_y, to_z):
        to_z = lax.rem(to_z + 2 * nz_, nz_)
        return (s + a, 2 * to_y + to_z // nc_, lax.rem(to_z, nc_))

    def half_at(at_z):
        return lax.rem(at_z + 2 * nz_, nz_) // nc_

    barrier = pltpu.get_barrier_semaphore()
    goes = [(k, 0, 0) for k in range(1, ns_)] + [(-1, 0, 0), (-1, 0, -1), (-1, 0, 1), (0, 0, -1), (0, 0, 1)]
    expected = 0
    for a, e in ((0, hop), (0, -hop), (-1, -hop)):
        for b in (-1, 0, 1):
            def both(sign, a=a, b=b):
                return (s + sign * a >= 0) & (s + sign * a < ns_) & (y + sign * b >= 0) & (y + sign * b < ny_)

            @pl.when(both(-1))
            def _(a=a, b=b, e=e):
                pl.semaphore_signal(barrier, inc=1, device_id=on_line(-a, y - b, z - e), device_id_type=MESH)

            expected = expected + both(1).astype(jnp.int32)
    for a, b, e in goes:
        @pl.when(inside(-a, -b, -e))
        def _(a=a, b=b, e=e):
            pl.semaphore_signal(barrier, inc=1, device_id=there(-a, -b, -e), device_id_type=MESH)

        expected = expected + inside(a, b, e).astype(jnp.int32)

    locals_ = [
        pltpu.make_async_copy(src, dst, lsem.at[k])
        for k, (src, dst) in enumerate(
            (
                (images.at[1], ext.at[0, HALF : HALF + TILE, N : N + TILE]),
                (images.at[0], own),
                (table, t),
                (off_in, off),
                (warp_in, warp),
                (stiff_in, stiff),
                (valid_in, valid),
            )
        )
    ]
    for copy in locals_:
        copy.start()

    @pl.when(r == 0)
    def _():
        for p in range(2):
            ext[p, 0:HALF, :] = jnp.zeros((HALF, TILE + 2 * N), F32)

    @pl.when(r == nr_ - 1)
    def _():
        for p in range(2):
            ext[p, HALF + TILE :, :] = jnp.zeros((HALF, TILE + 2 * N), F32)

    @pl.when(c == 0)
    def _():
        for p in range(2):
            ext[p, 0:HALF, 0:N] = jnp.zeros((HALF, N), F32)
            ext[p, HALF + TILE :, 0:N] = jnp.zeros((HALF, N), F32)
            landed[p, 0] = jnp.zeros((TILE // 2, N), F32)

    @pl.when(c == nc_ - 1)
    def _():
        for p in range(2):
            ext[p, 0:HALF, N + TILE :] = jnp.zeros((HALF, N), F32)
            ext[p, HALF + TILE :, N + TILE :] = jnp.zeros((HALF, N), F32)
            landed[p, 1] = jnp.zeros((TILE // 2, N), F32)

    @pl.when(s == ns_ - 1)
    def _():
        ext[1] = jnp.zeros((TILE + 2 * HALF, TILE + 2 * N), F32)
        landed[1] = jnp.zeros((2, TILE // 2, N), F32)

    near = [(b, e) for b in (1, -1, 0) for e in (0, -1, 1) if (b, e) != (0, 0)]
    blank = jnp.zeros((8, N), F32)
    for b, e in near:
        @pl.when(jnp.logical_not(inside(0, b, e)))
        def _(b=b, e=e):
            fslots[3 * (b + 1) + e + 1] = blank

    for k in range(ns_):
        @pl.when(s <= k)
        def _(k=k):
            dslots[k] = blank

    def pack(strip, side):
        count = strip.shape[0] // 2
        upper, lower = strip[:count], strip[count:]
        low = iota((count, N), 1) < HALF
        return jnp.where(low, swap(upper), lower) if side else jnp.where(low, upper, swap(lower))

    def unpack(got, side):
        turned = swap(got)
        return (got, turned) if side else (turned, got)

    def mine_spectra(p):
        def step(i, _):
            at = pl.multiple_of(i * N, N)
            if p == 0:
                blocks = [own[pl.ds(at, N), j * N : j * N + N] for j in range(SIDE)]
            else:
                at = pl.multiple_of(at + HALF, HALF)
                blocks = [ext[0, pl.ds(at, N), j * N + N : j * N + 2 * N] for j in range(SIDE)]
            found = forward(jnp.concatenate(blocks, 0), t)
            for j in range(SIDE):
                spec[9 * p + SIDE * i + j] = found[j * N : j * N + N]
            return 0

        lax.fori_loop(0, SIDE, step, 0)

    pl.semaphore_wait(barrier, expected)

    def remote(src, dst, send, recv, target):
        return pltpu.make_async_remote_copy(
            src_ref=src, dst_ref=dst, send_sem=send, recv_sem=recv, device_id=target, device_id_type=MESH
        )

    def col_rim(p, side):
        e = 2 * side - 1
        return remote(
            packed.at[1 - p, side], landed.at[p, 1 - side], cs.at[2 * p + side], cr.at[2 * p + 1 - side], there(-p, 0, e)
        )

    def tile_copy():
        return remote(images.at[0], ext.at[1, HALF : HALF + TILE, N : N + TILE], ts.at[0], tr.at[0], there(-1, 0, 0))

    turn_y = 2 * half - 1
    has_cross = (y + turn_y >= 0) & (y + turn_y < ny_)
    first_at, last_at = 0, HALF + TILE

    def takes(at_y):
        return ny_ - 1 - at_y

    def rows_of(kind):
        return HALF // PARTS[kind]

    def rim_at(kind, of_half):
        return of_half * last_at if kind else (1 - of_half) * last_at

    def leg(p, kind, k, m, block=None):
        sign = 1 - 2 * p
        n = rows_of(kind)
        index = (p * 2 + kind) * PARTS[1] + m
        index = index * (LEGS - 1) + k if block is None else 4 * PARTS[1] * (LEGS - 1) + index * SIDE + block
        lanes = slice(0, TILE) if block is None else slice(block * N, block * N + N)
        if k == 0:
            top = pl.multiple_of((half if kind else 1 - half) * (TILE - HALF) + m * n, 8)
            src = images.at[1 - p, pl.ds(top, n), :]
            to_y = y
            if kind:
                early = ((half == 1) & (m >= takes(y))) | ((half == 0) & (m < takes(y - 1)))
                to_y = jnp.where(early, y + turn_y, y)
            target = on_line(-p, to_y, z + sign * hop)
        else:
            src = transit.at[p, kind, k - 1, pl.ds(m * n, n), lanes]
            to_y = y
            if kind and k == LEGS - 1:
                from_half = half_at(z - sign * hop * k)
                late = ((from_half == 1) & (m < takes(y))) | ((from_half == 0) & (m > takes(y)))
                to_y = jnp.where(late, y + 2 * from_half - 1, y)
            target = on_line(0, to_y, z + sign * hop)
        if k == LEGS - 1:
            at = pl.multiple_of(rim_at(kind, half_at(z + sign * hop)) + m * n, 8)
            dst = ext.at[p, pl.ds(at, n), lanes.start + N : lanes.stop + N]
        else:
            dst = transit.at[p, kind, k, pl.ds(m * n, n), :]
        return remote(src, dst, rs.at[index], rr.at[index], target)

    def leg_comes(p, kind, k, m):
        ok = s + p < ns_
        if kind:
            ok = ok & (has_cross if k == LEGS - 1 else m != takes(y))
        return ok

    def leg_goes(p, kind, k, m):
        if k:
            return leg_comes(p, kind, k - 1, m)
        return (s - p >= 0) & has_cross if kind else s - p >= 0

    def begin(kind, pairs=(0, 1)):
        for m in range(PARTS[kind]):
            for p in pairs:
                @pl.when(leg_goes(p, kind, 0, m))
                def _(p=p, m=m):
                    leg(p, kind, 0, m).start()

    def each_part(kind, condition, k, act):
        for m in range(PARTS[kind]):
            for p in range(2):
                @pl.when(condition(p, kind, k, m))
                def _(p=p, m=m):
                    act(p, m)

    def pass_on(kind, k):
        def act(p, m):
            leg(p, kind, k, m).wait_recv()
            if k < LEGS - 2:
                leg(p, kind, k + 1, m).start()
            else:
                leg(p, kind, k + 1, m, 0).start()
                leg(p, kind, k + 1, m, SIDE - 1).start()

        each_part(kind, leg_comes, k, act)
        if k == LEGS - 2:
            each_part(kind, leg_comes, k, lambda p, m: leg(p, kind, k + 1, m, 1).start())

    def arrive(kind, blocks):
        def act(p, m):
            for block in blocks:
                leg(p, kind, LEGS - 1, m, block).wait_recv()

        each_part(kind, leg_comes, LEGS - 1, act)

    def corner(p, kind, side):
        n = 4 * p + 2 * kind
        return remote(
            cpacked.at[p, kind, side],
            clanded.at[p, kind, 1 - side],
            ks.at[n + side],
            kr.at[n + 1 - side],
            there(0, 0, 2 * side - 1),
        )

    def rim_rows(kind):
        return pl.ds(pl.multiple_of(rim_at(kind, half), HALF), HALF)

    def corner_moves(p, kind, e):
        ok = (s + p < ns_) & inside(0, 0, e)
        return ok & has_cross if kind else ok

    def send_corners(kind):
        for p in range(2):
            for side in range(2):
                @pl.when(corner_moves(p, kind, 2 * side - 1))
                def _(p=p, side=side):
                    src = slice(TILE, TILE + N) if side else slice(N, 2 * N)
                    cpacked[p, kind, side] = pack(ext[p, rim_rows(kind), src], side)
                    corner(p, kind, side).start()

    def await_corners(kind, p):
        for side in range(2):
            @pl.when(corner_moves(p, kind, 1 - 2 * side))
            def _(side=side):
                corner(p, kind, side).wait_recv()
                dst = slice(0, N) if side else slice(N + TILE, 2 * N + TILE)
                ext[p, rim_rows(kind), dst] = jnp.concatenate(unpack(clanded[p, kind, 1 - side], 1 - side), 0)

    def frame_copy(b, e):
        n, m = 3 * (b + 1) + e + 1, 3 * (1 - b) + 1 - e
        return remote(ftile, fslots.at[m], fs.at[n], fr.at[m], there(0, b, e))

    def match(vertices):
        lane = iota((N, N), 1)
        row = iota((N, N), 0)
        low = lane < HALF
        found = dtile[...]
        stack = []
        for p, i, j in vertices:
            top = i * N

            def at(first, rows, block):
                if not isinstance(i, int):
                    first = pl.multiple_of(first, HALF)
                return ext[p, pl.ds(first, rows), block * N : block * N + N]

            def beside(first, rows):
                left, right = at(first, rows, j), at(first, rows, j + 2)
                return jnp.where(low[:rows], right, left)

            dy, dx = off[0, i, p, j], off[1, i, p, j]
            in_rows = (row >= dy) & (row < dy + N)
            in_cols = (lane >= dx) & (lane < dx + N)
            main = jnp.where(in_cols, at(top + HALF, N, j + 1), beside(top + HALF, N))
            over = jnp.concatenate([at(top + HALF + N, HALF, j + 1), at(top, HALF, j + 1)], 0)
            over_side = jnp.concatenate([beside(top + HALF + N, HALF), beside(top, HALF)], 0)
            stack.append(jnp.where(in_rows, main, jnp.where(in_cols, over, over_side)))
        theirs = forward(jnp.concatenate(stack, 0), t)
        scores = inverse(
            jnp.concatenate(
                [cross(spec[9 * p + SIDE * i + j], theirs[k * N : k * N + N]) for k, (p, i, j) in enumerate(vertices)], 0
            ),
            t,
        )
        shifts = [(off[0, i, p, j], off[1, i, p, j]) for p, i, j in vertices]
        for comp, found_shifts in enumerate(peaks(scores, shifts)):
            for k, (p, i, j) in enumerate(vertices):
                value = (shifts[k][comp].astype(F32) + found_shifts[k : k + 1]) * (1.0 / N)
                found = jnp.where((row8 == i) & (lane8 == 16 * (2 * comp + p) + j), value, found)
        dtile[...] = found

    def match_row(p, i):
        match([(p, i, j) for j in range(SIDE)])

    def fill_columns(p):
        for side in range(2):
            @pl.when(inside(p, 0, 1 - 2 * side))
            def _(side=side):
                col_rim(p, side).wait_recv()
        for side in range(2):
            column = slice(0, N) if side == 0 else slice(N + TILE, 2 * N + TILE)
            upper, lower = unpack(landed[p, side], side)
            ext[p, HALF : HALF + TILE // 2, column] = upper
            ext[p, HALF + TILE // 2 : HALF + TILE, column] = lower

    begin(0)
    begin(1)

    @pl.when(s > 0)
    def _():
        tile_copy().start()

    for copy in locals_[:2]:
        copy.wait()
    for im in range(2):
        for side in range(2):
            if im == 0:
                strip = own[:, 0:N] if side == 0 else own[:, TILE - N :]
            else:
                strip = ext[0, HALF : HALF + TILE, N : 2 * N] if side == 0 else ext[0, HALF : HALF + TILE, TILE : TILE + N]
            packed[im, side] = pack(strip, side)
    for p in (0, 1):
        for side in range(2):
            @pl.when(inside(-p, 0, 2 * side - 1))
            def _(p=p, side=side):
                col_rim(p, side).start()

    for copy in locals_[2:]:
        copy.wait()
    mine_spectra(0)
    pass_on(0, 0)
    pass_on(1, 0)
    row8, lane8 = iota((8, N), 0), iota((8, N), 1)
    small[...] = jnp.zeros_like(small)
    for comp in range(2):
        for sec in range(2):
            small[2 * comp + sec, 0:SIDE, 0:SIDE] = warp[comp, :, sec]
            small[4 + 2 * comp + sec, 0:SIDE, 0:SIDE] = stiff[comp, :, sec]
    for sec in range(2):
        small[8 + sec, 0:SIDE, 0:SIDE] = ANCHOR * valid[:, sec].astype(F32)
    dtile[...] = blank
    start = jnp.zeros((8, N), F32)
    held = jnp.zeros((8, N), F32)
    for g in range(4):
        sec = g % 2
        w = small[g]
        right = jnp.where((c == nc_ - 1) & (lane8 == SIDE - 1), 0.0, small[4 + sec])
        down = jnp.where((r == nr_ - 1) & (row8 == SIDE - 1), 0.0, small[6 + sec])
        start = start + (pltpu.roll(w, 16 * g, 1) if g else w)
        for q, quantity in enumerate((w, right, down, small[8 + sec])):
            by = 16 * g + SIDE * q
            held = held + (pltpu.roll(quantity, by, 1) if by else quantity)

    mine_spectra(1)
    fill_columns(0)
    for k in range(1, LEGS - 1):
        pass_on(0, k)
        pass_on(1, k)
        if k == 1:
            match_row(0, 1)
    if LEGS < 3:
        match_row(0, 1)

    @pl.when(s < ns_ - 1)
    def _():
        tile_copy().wait_recv()

    fill_columns(1)
    match_row(1, 1)
    along, across = 2 * (1 - half), 2 * half
    arrive(0, (0, SIDE - 1))
    send_corners(0)
    arrive(0, (1,))
    match([(p, along, 1) for p in range(2)])
    arrive(1, (0, SIDE - 1))
    send_corners(1)
    arrive(1, (1,))
    for p in range(2):
        await_corners(0, p)
    match([(p, across, 1) for p in range(2)] + [(p, along, j) for p in range(2) for j in (0, 2)])
    for p in range(2):
        await_corners(1, p)
    match([(p, across, j) for p in range(2) for j in (0, 2)])

    silent = (s == ns_ - 1) & ((lane8 & 16) != 0)
    found = jnp.where(silent, 0.0, dtile[...])
    dtile[...] = found

    def total_copy(k):
        return remote(dtile, dslots.at[s], ds.at[k], dr.at[s], (k, r, c))

    def total_arrival(k):
        return remote(dtile, dslots.at[k], ds.at[k], dr.at[k], (k, r, c))

    for k in range(ns_ - 1, 0, -1):
        @pl.when(k > s)
        def _(k=k):
            total_copy(k).start()
    for g in range(4):
        out_ref[0, g // 2, :, g % 2] = (pltpu.roll(found, N - 16 * g, 1) if g else found)[0:SIDE, 0:SIDE]
    strips[...] = jnp.zeros_like(strips)

    for k in range(ns_ - 1):
        @pl.when(k < s)
        def _(k=k):
            total_arrival(k).wait_recv()
    lower = dslots[0]
    for k in range(1, ns_ - 1):
        lower = lower + dslots[k]
    second = (lane8 & 16) != 0
    below = lower + jnp.where(second, pltpu.roll(lower, 16, 1), pltpu.roll(lower, N - 16, 1))
    below = below + jnp.where(second, pltpu.roll(found, 16, 1), 0.0)
    ftile[...] = held + pltpu.roll(start - below, 4 * SIDE, 1)
    for b, e in near:
        @pl.when(inside(0, b, e))
        def _(b=b, e=e):
            frame_copy(b, e).start()

    for p in (0, 1):
        for side in range(2):
            @pl.when(inside(-p, 0, 2 * side - 1))
            def _(p=p, side=side):
                col_rim(p, side).wait_send()

            for kind in range(2):
                @pl.when(corner_moves(p, kind, 2 * side - 1))
                def _(p=p, kind=kind, side=side):
                    corner(p, kind, side).wait_send()

        for kind in range(2):
            for k in range(LEGS):
                for m in range(PARTS[kind]):
                    @pl.when(leg_goes(p, kind, k, m))
                    def _(p=p, kind=kind, k=k, m=m):
                        for block in range(SIDE) if k == LEGS - 1 else (None,):
                            leg(p, kind, k, m, block).wait_send()

    @pl.when(s > 0)
    def _():
        tile_copy().wait_send()

    for k in range(1, ns_):
        @pl.when(k > s)
        def _(k=k):
            total_copy(k).wait_send()
    for b, e in near:
        @pl.when(inside(0, b, e))
        def _(b=b, e=e):
            frame_copy(b, e).wait_send()
            frame_copy(-b, -e).wait_recv()

    for b in (-1, 0, 1):
        for e in (-1, 0, 1):
            at = SIDE * (b + 1)
            tile = ftile[...] if (b, e) == (0, 0) else fslots[3 * (b + 1) + e + 1]
            strips[e + 1, at : at + SIDE, :] = tile[0:SIDE]
    lane16 = iota((16, N), 1) & 15

    def frame(q):
        out = jnp.zeros((16, N), F32)
        for e in (-1, 0, 1):
            at = SIDE * (e + 1)
            by = (at - SIDE * q) % N
            strip = strips[e + 1]
            strip = pltpu.roll(strip, by, 1) if by else strip
            out = jnp.where((lane16 >= at) & (lane16 < at + SIDE), strip, out)
        return out

    v, right, down, anchor, target = (frame(q) for q in range(5))
    right_left = pltpu.roll(right, 1, 1)
    down_upper = pltpu.roll(down, 1, 0)
    for _ in range(ITERS):
        v = (
            v
            + right * (pltpu.roll(v, N - 1, 1) - v)
            + right_left * (pltpu.roll(v, 1, 1) - v)
            + down * (pltpu.roll(v, 15, 0) - v)
            + down_upper * (pltpu.roll(v, 1, 0) - v)
            + anchor * (target - v)
        )
    v = pltpu.roll(v, 16 - SIDE, 0)
    for g in range(4):
        out_ref[1, g // 2, :, g % 2] = pltpu.roll(v, (N - 16 * g - SIDE) % N, 1)[0:SIDE, 0:SIDE]


def per_device(sizes, images, offsets, warp, stiffness, valid):
    vmem = pl.BlockSpec(memory_space=pltpu.VMEM)
    anywhere = pl.BlockSpec(memory_space=pl.ANY)
    dma = pltpu.SemaphoreType.DMA
    out = jax.ShapeDtypeStruct((2, 2, SIDE, 2, SIDE), F32)
    n = sizes[0]
    turned = (0, 2, 1, 3)
    outs = pl.pallas_call(
        functools.partial(kernel, sizes),
        name="align",
        out_shape=out,
        in_specs=[anywhere] * 6,
        out_specs=vmem,
        scratch_shapes=[
            pltpu.SMEM((2, SIDE, 2, SIDE), jnp.int32),
            pltpu.VMEM((2, SIDE, 2, SIDE), F32),
            pltpu.VMEM((2, SIDE, 2, SIDE), F32),
            pltpu.VMEM((SIDE, 2, SIDE), jnp.int32),
            pltpu.VMEM((2 * N, 6 * N), BF),
            pltpu.VMEM((TILE, TILE), F32),
            pltpu.VMEM((2, TILE + 2 * HALF, TILE + 2 * N), F32),
            pltpu.VMEM((18, N, N), F32),
            pltpu.VMEM((2, 2, TILE // 2, N), F32),
            pltpu.VMEM((2, 2, TILE // 2, N), F32),
            pltpu.VMEM((2, 2, LEGS - 1, HALF, TILE), F32),
            pltpu.VMEM((2, 2, 2, HALF // 2, N), F32),
            pltpu.VMEM((2, 2, 2, HALF // 2, N), F32),
            pltpu.VMEM((10, 8, N), F32),
            pltpu.VMEM((8, N), F32),
            pltpu.VMEM((9, 8, N), F32),
            pltpu.VMEM((8, N), F32),
            pltpu.VMEM((n, 8, N), F32),
            pltpu.VMEM((3, 16, N), F32),
            dma((7,)),
            dma((1,)),
            dma((1,)),
            dma((4 * PARTS[1] * (LEGS + 2),)),
            dma((4 * PARTS[1] * (LEGS + 2),)),
            dma((4,)),
            dma((4,)),
            dma((8,)),
            dma((8,)),
            dma((n,)),
            dma((n,)),
            dma((9,)),
            dma((9,)),
        ],
        compiler_params=pltpu.CompilerParams(
            collective_id=0, has_side_effects=True, vmem_limit_bytes=60 * 1024 * 1024
        ),
    )(
        images,
        offsets.transpose(turned),
        warp.transpose(turned),
        stiffness.transpose(turned),
        valid.transpose(1, 0, 2),
        jnp.asarray(tables()),
    )
    return tuple(x.transpose(turned) for x in outs)


def solution(mesh):
    sizes = tuple(mesh.shape[a] for a in ("sec", "row", "col"))
    return jax.shard_map(
        functools.partial(per_device, sizes),
        mesh=mesh,
        in_specs=(
            P("sec", "row", "col"),
            P(None, "sec", "row", "col"),
            P(None, "sec", "row", "col"),
            P(None, "sec", "row", "col"),
            P("sec", "row", "col"),
        ),
        out_specs=(P(None, "sec", "row", "col"), P(None, "sec", "row", "col")),
        check_vma=False,
    )
```

```python
import functools

import jax
import jax.numpy as jnp
import ml_dtypes
import numpy as np
from jax import lax
from jax.experimental import pallas as pl
from jax.experimental.pallas import tpu as pltpu
from jax.sharding import PartitionSpec as P

MESH = pl.DeviceIdType.MESH
N = 128
HALF = 64
SIDE = 3
TILE = SIDE * N
BLOCKS = 2 * TILE // N
SHARPNESS = 80.0
ANCHOR = 0.2
ITERS = 3
LEGS = 4
PARTS = (4, 4)
BF = jnp.bfloat16
F32 = jnp.float32


def split3(a):
    high = a.astype(ml_dtypes.bfloat16)
    rest = a - high.astype(np.float64)
    mid = rest.astype(ml_dtypes.bfloat16)
    low = (rest - mid.astype(np.float64)).astype(ml_dtypes.bfloat16)
    return high, mid, low


def tables():
    x = np.arange(N)
    forward = np.zeros((N, N))
    for f in range(HALF):
        forward[f] = np.cos(2 * np.pi * ((f * x) % N) / N)
    forward[HALF] = 1 - 2 * (x % 2)
    for f in range(1, HALF):
        forward[HALF + f] = np.sin(2 * np.pi * ((f * x) % N) / N)
    scale = np.full(N, 2.0 / N)
    scale[0] = scale[HALF] = 1.0 / N
    inverse = (forward * scale[:, None]).T

    def right(a):
        h, m, l = split3(a)
        return np.block([[h, m], [h, m]]), np.concatenate([h, l], 0)

    return np.concatenate([*right(forward.T), *right(inverse.T * np.sqrt(SHARPNESS / (N * N)))], 1)


def parts(x):
    high = x.astype(BF)
    rest = x - high.astype(F32)
    mid = rest.astype(BF)
    low = (rest - mid.astype(F32)).astype(BF)
    return high, mid, low


def dot(a, b):
    return jnp.dot(a, b, preferred_element_type=F32)


def right_mul(x, wa, wb):
    high, mid, low = parts(x)
    a = dot(jnp.concatenate([high, mid], 1), wa)
    return a[:, :N] + a[:, N:] + dot(jnp.concatenate([low, high], 1), wb)


def turn(x):
    return jnp.concatenate([x[k : k + N].T for k in range(0, x.shape[0], N)], 0)


def forward(x, t):
    return right_mul(turn(right_mul(x, t[:, 0 : 2 * N], t[:, 2 * N : 3 * N])), t[:, 0 : 2 * N], t[:, 2 * N : 3 * N])


def inverse(x, t):
    return right_mul(turn(right_mul(x, t[:, 3 * N : 5 * N], t[:, 5 * N :])), t[:, 3 * N : 5 * N], t[:, 5 * N :])


def iota(shape, dim):
    return lax.broadcasted_iota(jnp.int32, shape, dim)


def swap(x):
    return pltpu.roll(x, HALF, 1)


def cross(mine, theirs):
    lane = iota((N, N), 1)
    single = (lane & (HALF - 1)) == 0
    turned = swap(theirs)
    first = jnp.where(single | (lane < HALF), theirs, -turned)
    second = jnp.where(single, 0.0, jnp.where(lane < HALF, turned, theirs))
    other = swap(mine)
    even, odd = slice(0, HALF), slice(HALF, N)

    def pair(a, b):
        return mine[a] * first[b] + other[a] * second[b]

    lone = iota((HALF, N), 0) == 0
    both = pair(odd, odd)
    top = pair(even, even) + jnp.where(lone, 0.0, both)
    top = jnp.where(lone & (iota((HALF, N), 1) == 0), 0.0, top)
    low = jnp.where(lone, both, pair(even, odd) - pair(odd, even))
    return jnp.concatenate([top, low], 0)


def peaks(scores, shifts):
    count = len(shifts)
    blocks = [scores[k * N : k * N + N] for k in range(count)]
    highest = jnp.concatenate([jnp.max(x, axis=0, keepdims=True) for x in blocks], 0)
    highest = jnp.max(highest, axis=1, keepdims=True)
    sums = []
    for k, (dy, dx) in enumerate(shifts):
        rows = (((iota((N, N), 0) - dy + HALF) & (N - 1)) - HALF).astype(F32)
        cols = (((iota((1, N), 1) - dx + HALF) & (N - 1)) - HALF).astype(F32)
        weights = jnp.exp(blocks[k] - highest[k : k + 1])
        by_col = jnp.sum(weights, axis=0, keepdims=True)
        sums.append((by_col, jnp.sum(weights * rows, axis=0, keepdims=True), by_col * cols))
    sums = [jnp.sum(jnp.concatenate([x[q] for x in sums], 0), axis=1, keepdims=True) for q in range(3)]
    return sums[1] / sums[0], sums[2] / sums[0]


class Remote:
    def __init__(self, src, dst, send, recv, target, here):
        self.refs, self.target, self.here = (src, dst, send, recv), target, here

    def to(self, device):
        return pltpu.make_async_remote_copy(*self.refs, device_id=device, device_id_type=MESH)

    def start(self):
        self.to(self.target).start()

    def wait_recv(self):
        self.to(self.here).wait_recv()

    def wait_send(self):
        self.to(self.here).wait_send()


def kernel(sizes, images, off_in, warp_in, stiff_in, valid_in, table, out_ref, *rest):
    (off, warp, stiff, valid, t, own, ext, spec, packed, landed, transit, cpacked, clanded) = rest[:13]
    (small, ftile, fslots, dtile, dslots, strips) = rest[13:19]
    lsem, ts, tr, rs, rr, cs, cr, ks, kr, ds, dr, fs, fr = rest[19:]
    ns_, nr_, nc_ = sizes
    ny_, nz_ = nr_ // 2, 2 * nc_
    hop = nc_ // LEGS
    s, r, c = lax.axis_index("sec"), lax.axis_index("row"), lax.axis_index("col")
    y, half = r // 2, lax.rem(r, 2)
    z = half * nc_ + c

    def inside(a, b, e):
        ok = None
        for at, by, n in ((s, a, ns_), (r, b, nr_), (c, e, nc_)):
            if by:
                here = (at + by >= 0) & (at + by < n)
                ok = here if ok is None else ok & here
        return ok

    def there(a, b, e):
        return (s + a, r + b, c + e)

    def on_line(a, to_y, to_z):
        to_z = lax.rem(to_z + 2 * nz_, nz_)
        return (s + a, 2 * to_y + to_z // nc_, lax.rem(to_z, nc_))

    def half_at(at_z):
        return lax.rem(at_z + 2 * nz_, nz_) // nc_

    barrier = pltpu.get_barrier_semaphore()
    goes = [(k, 0, 0) for k in range(1, ns_)] + [(-1, 0, 0), (-1, 0, -1), (-1, 0, 1), (0, 0, -1), (0, 0, 1)]
    expected = 0
    for a, e in ((0, hop), (0, -hop), (-1, -hop)):
        for b in (-1, 0, 1):
            def both(sign, a=a, b=b):
                return (s + sign * a >= 0) & (s + sign * a < ns_) & (y + sign * b >= 0) & (y + sign * b < ny_)

            @pl.when(both(-1))
            def _(a=a, b=b, e=e):
                pl.semaphore_signal(barrier, inc=1, device_id=on_line(-a, y - b, z - e), device_id_type=MESH)

            expected = expected + both(1).astype(jnp.int32)
    for a, b, e in goes:
        @pl.when(inside(-a, -b, -e))
        def _(a=a, b=b, e=e):
            pl.semaphore_signal(barrier, inc=1, device_id=there(-a, -b, -e), device_id_type=MESH)

        expected = expected + inside(a, b, e).astype(jnp.int32)

    locals_ = [
        pltpu.make_async_copy(src, dst, lsem.at[k])
        for k, (src, dst) in enumerate(
            (
                (images.at[1], ext.at[0, HALF : HALF + TILE, N : N + TILE]),
                (images.at[0], own),
                (table, t),
                (off_in, off),
                (warp_in, warp),
                (stiff_in, stiff),
                (valid_in, valid),
            )
        )
    ]
    for copy in locals_:
        copy.start()

    @pl.when(r == 0)
    def _():
        for p in range(2):
            ext[p, 0:HALF, :] = jnp.zeros((HALF, TILE + 2 * N), F32)

    @pl.when(r == nr_ - 1)
    def _():
        for p in range(2):
            ext[p, HALF + TILE :, :] = jnp.zeros((HALF, TILE + 2 * N), F32)

    @pl.when(c == 0)
    def _():
        for p in range(2):
            ext[p, 0:HALF, 0:N] = jnp.zeros((HALF, N), F32)
            ext[p, HALF + TILE :, 0:N] = jnp.zeros((HALF, N), F32)
            landed[p, 0] = jnp.zeros((TILE // 2, N), F32)

    @pl.when(c == nc_ - 1)
    def _():
        for p in range(2):
            ext[p, 0:HALF, N + TILE :] = jnp.zeros((HALF, N), F32)
            ext[p, HALF + TILE :, N + TILE :] = jnp.zeros((HALF, N), F32)
            landed[p, 1] = jnp.zeros((TILE // 2, N), F32)

    @pl.when(s == ns_ - 1)
    def _():
        ext[1] = jnp.zeros((TILE + 2 * HALF, TILE + 2 * N), F32)
        landed[1] = jnp.zeros((2, TILE // 2, N), F32)

    near = [(b, e) for b in (1, -1, 0) for e in (0, -1, 1) if (b, e) != (0, 0)]
    blank = jnp.zeros((8, N), F32)
    for b, e in near:
        @pl.when(jnp.logical_not(inside(0, b, e)))
        def _(b=b, e=e):
            fslots[3 * (b + 1) + e + 1] = blank

    for k in range(ns_):
        @pl.when(s <= k)
        def _(k=k):
            dslots[k] = blank

    def pack(strip, side):
        count = strip.shape[0] // 2
        upper, lower = strip[:count], strip[count:]
        low = iota((count, N), 1) < HALF
        return jnp.where(low, swap(upper), lower) if side else jnp.where(low, upper, swap(lower))

    def unpack(got, side):
        turned = swap(got)
        return (got, turned) if side else (turned, got)

    def mine_spectra(p):
        def step(i, _):
            at = pl.multiple_of(i * N, N)
            if p == 0:
                blocks = [own[pl.ds(at, N), j * N : j * N + N] for j in range(SIDE)]
            else:
                at = pl.multiple_of(at + HALF, HALF)
                blocks = [ext[0, pl.ds(at, N), j * N + N : j * N + 2 * N] for j in range(SIDE)]
            found = forward(jnp.concatenate(blocks, 0), t)
            for j in range(SIDE):
                spec[9 * p + SIDE * i + j] = found[j * N : j * N + N]
            return 0

        lax.fori_loop(0, SIDE, step, 0)

    pl.semaphore_wait(barrier, expected)

    def remote(src, dst, send, recv, target):
        return Remote(src, dst, send, recv, target, (s, r, c))

    def col_rim(p, side):
        e = 2 * side - 1
        return remote(
            packed.at[1 - p, side], landed.at[p, 1 - side], cs.at[2 * p + side], cr.at[2 * p + 1 - side], there(-p, 0, e)
        )

    def tile_copy():
        return remote(images.at[0], ext.at[1, HALF : HALF + TILE, N : N + TILE], ts.at[0], tr.at[0], there(-1, 0, 0))

    turn_y = 2 * half - 1
    has_cross = (y + turn_y >= 0) & (y + turn_y < ny_)
    first_at, last_at = 0, HALF + TILE

    def takes(at_y):
        return ny_ - 1 - at_y

    def rows_of(kind):
        return HALF // PARTS[kind]

    def rim_at(kind, of_half):
        return of_half * last_at if kind else (1 - of_half) * last_at

    def leg(p, kind, k, m, block=None):
        sign = 1 - 2 * p
        n = rows_of(kind)
        index = (p * 2 + kind) * PARTS[1] + m
        index = index * (LEGS - 1) + k if block is None else 4 * PARTS[1] * (LEGS - 1) + index * SIDE + block
        lanes = slice(0, TILE) if block is None else slice(block * N, block * N + N)
        if k == 0:
            top = pl.multiple_of((half if kind else 1 - half) * (TILE - HALF) + m * n, 8)
            src = images.at[1 - p, pl.ds(top, n), :]
            to_y = y
            if kind:
                early = ((half == 1) & (m >= takes(y))) | ((half == 0) & (m < takes(y - 1)))
                to_y = jnp.where(early, y + turn_y, y)
            target = on_line(-p, to_y, z + sign * hop)
        else:
            src = transit.at[p, kind, k - 1, pl.ds(m * n, n), lanes]
            to_y = y
            if kind and k == LEGS - 1:
                from_half = half_at(z - sign * hop * k)
                late = ((from_half == 1) & (m < takes(y))) | ((from_half == 0) & (m > takes(y)))
                to_y = jnp.where(late, y + 2 * from_half - 1, y)
            target = on_line(0, to_y, z + sign * hop)
        if k == LEGS - 1:
            at = pl.multiple_of(rim_at(kind, half_at(z + sign * hop)) + m * n, 8)
            dst = ext.at[p, pl.ds(at, n), lanes.start + N : lanes.stop + N]
        else:
            dst = transit.at[p, kind, k, pl.ds(m * n, n), :]
        return remote(src, dst, rs.at[index], rr.at[index], target)

    def leg_comes(p, kind, k, m):
        ok = s + p < ns_
        if kind:
            ok = ok & (has_cross if k == LEGS - 1 else m != takes(y))
        return ok

    def leg_goes(p, kind, k, m):
        if k:
            return leg_comes(p, kind, k - 1, m)
        return (s - p >= 0) & has_cross if kind else s - p >= 0

    def begin(kind, pairs=(0, 1)):
        for m in range(PARTS[kind]):
            for p in pairs:
                @pl.when(leg_goes(p, kind, 0, m))
                def _(p=p, m=m):
                    leg(p, kind, 0, m).start()

    def each_part(kind, condition, k, act):
        for m in range(PARTS[kind]):
            for p in range(2):
                @pl.when(condition(p, kind, k, m))
                def _(p=p, m=m):
                    act(p, m)

    def pass_on(kind, k):
        def act(p, m):
            leg(p, kind, k, m).wait_recv()
            if k < LEGS - 2:
                leg(p, kind, k + 1, m).start()
            else:
                leg(p, kind, k + 1, m, 0).start()
                leg(p, kind, k + 1, m, SIDE - 1).start()

        each_part(kind, leg_comes, k, act)
        if k == LEGS - 2:
            each_part(kind, leg_comes, k, lambda p, m: leg(p, kind, k + 1, m, 1).start())

    def arrive(kind, blocks):
        def act(p, m):
            for block in blocks:
                leg(p, kind, LEGS - 1, m, block).wait_recv()

        each_part(kind, leg_comes, LEGS - 1, act)

    def corner(p, kind, side):
        n = 4 * p + 2 * kind
        return remote(
            cpacked.at[p, kind, side],
            clanded.at[p, kind, 1 - side],
            ks.at[n + side],
            kr.at[n + 1 - side],
            there(0, 0, 2 * side - 1),
        )

    def rim_rows(kind):
        return pl.ds(pl.multiple_of(rim_at(kind, half), HALF), HALF)

    def corner_moves(p, kind, e):
        ok = (s + p < ns_) & inside(0, 0, e)
        return ok & has_cross if kind else ok

    def send_corners(kind):
        for p in range(2):
            for side in range(2):
                @pl.when(corner_moves(p, kind, 2 * side - 1))
                def _(p=p, side=side):
                    src = slice(TILE, TILE + N) if side else slice(N, 2 * N)
                    cpacked[p, kind, side] = pack(ext[p, rim_rows(kind), src], side)
                    corner(p, kind, side).start()

    def await_corners(kind, p):
        for side in range(2):
            @pl.when(corner_moves(p, kind, 1 - 2 * side))
            def _(side=side):
                corner(p, kind, side).wait_recv()
                dst = slice(0, N) if side else slice(N + TILE, 2 * N + TILE)
                ext[p, rim_rows(kind), dst] = jnp.concatenate(unpack(clanded[p, kind, 1 - side], 1 - side), 0)

    def frame_copy(b, e):
        n, m = 3 * (b + 1) + e + 1, 3 * (1 - b) + 1 - e
        return remote(ftile, fslots.at[m], fs.at[n], fr.at[m], there(0, b, e))

    def match(vertices):
        lane = iota((N, N), 1)
        row = iota((N, N), 0)
        low = lane < HALF
        found = dtile[...]
        stack = []
        for p, i, j in vertices:
            top = i * N

            def at(first, rows, block):
                if not isinstance(i, int):
                    first = pl.multiple_of(first, HALF)
                return ext[p, pl.ds(first, rows), block * N : block * N + N]

            def beside(first, rows):
                left, right = at(first, rows, j), at(first, rows, j + 2)
                return jnp.where(low[:rows], right, left)

            dy, dx = off[0, i, p, j], off[1, i, p, j]
            in_rows = (row >= dy) & (row < dy + N)
            in_cols = (lane >= dx) & (lane < dx + N)
            main = jnp.where(in_cols, at(top + HALF, N, j + 1), beside(top + HALF, N))
            over = jnp.concatenate([at(top + HALF + N, HALF, j + 1), at(top, HALF, j + 1)], 0)
            over_side = jnp.concatenate([beside(top + HALF + N, HALF), beside(top, HALF)], 0)
            stack.append(jnp.where(in_rows, main, jnp.where(in_cols, over, over_side)))
        theirs = forward(jnp.concatenate(stack, 0), t)
        scores = inverse(
            jnp.concatenate(
                [cross(spec[9 * p + SIDE * i + j], theirs[k * N : k * N + N]) for k, (p, i, j) in enumerate(vertices)], 0
            ),
            t,
        )
        shifts = [(off[0, i, p, j], off[1, i, p, j]) for p, i, j in vertices]
        for comp, found_shifts in enumerate(peaks(scores, shifts)):
            for k, (p, i, j) in enumerate(vertices):
                value = (shifts[k][comp].astype(F32) + found_shifts[k : k + 1]) * (1.0 / N)
                found = jnp.where((row8 == i) & (lane8 == 16 * (2 * comp + p) + j), value, found)
        dtile[...] = found

    def match_row(p, i):
        match([(p, i, j) for j in range(SIDE)])

    def fill_columns(p):
        for side in range(2):
            @pl.when(inside(p, 0, 1 - 2 * side))
            def _(side=side):
                col_rim(p, side).wait_recv()
        for side in range(2):
            column = slice(0, N) if side == 0 else slice(N + TILE, 2 * N + TILE)
            upper, lower = unpack(landed[p, side], side)
            ext[p, HALF : HALF + TILE // 2, column] = upper
            ext[p, HALF + TILE // 2 : HALF + TILE, column] = lower

    begin(0)
    begin(1)

    @pl.when(s > 0)
    def _():
        tile_copy().start()

    for copy in locals_[:2]:
        copy.wait()
    for im in range(2):
        for side in range(2):
            if im == 0:
                strip = own[:, 0:N] if side == 0 else own[:, TILE - N :]
            else:
                strip = ext[0, HALF : HALF + TILE, N : 2 * N] if side == 0 else ext[0, HALF : HALF + TILE, TILE : TILE + N]
            packed[im, side] = pack(strip, side)
    for p in (0, 1):
        for side in range(2):
            @pl.when(inside(-p, 0, 2 * side - 1))
            def _(p=p, side=side):
                col_rim(p, side).start()

    for copy in locals_[2:]:
        copy.wait()
    mine_spectra(0)
    pass_on(0, 0)
    pass_on(1, 0)
    row8, lane8 = iota((8, N), 0), iota((8, N), 1)
    small[...] = jnp.zeros_like(small)
    for comp in range(2):
        for sec in range(2):
            small[2 * comp + sec, 0:SIDE, 0:SIDE] = warp[comp, :, sec]
            small[4 + 2 * comp + sec, 0:SIDE, 0:SIDE] = stiff[comp, :, sec]
    for sec in range(2):
        small[8 + sec, 0:SIDE, 0:SIDE] = ANCHOR * valid[:, sec].astype(F32)
    dtile[...] = blank
    start = jnp.zeros((8, N), F32)
    held = jnp.zeros((8, N), F32)
    for g in range(4):
        sec = g % 2
        w = small[g]
        right = jnp.where((c == nc_ - 1) & (lane8 == SIDE - 1), 0.0, small[4 + sec])
        down = jnp.where((r == nr_ - 1) & (row8 == SIDE - 1), 0.0, small[6 + sec])
        start = start + (pltpu.roll(w, 16 * g, 1) if g else w)
        for q, quantity in enumerate((w, right, down, small[8 + sec])):
            by = 16 * g + SIDE * q
            held = held + (pltpu.roll(quantity, by, 1) if by else quantity)

    mine_spectra(1)
    fill_columns(0)
    for k in range(1, LEGS - 1):
        pass_on(0, k)
        pass_on(1, k)
        if k == 1:
            match_row(0, 1)
    if LEGS < 3:
        match_row(0, 1)

    @pl.when(s < ns_ - 1)
    def _():
        tile_copy().wait_recv()

    fill_columns(1)
    match_row(1, 1)
    along, across = 2 * (1 - half), 2 * half
    arrive(0, (0, SIDE - 1))
    send_corners(0)
    arrive(0, (1,))
    match([(p, along, 1) for p in range(2)])
    arrive(1, (0, SIDE - 1))
    send_corners(1)
    arrive(1, (1,))
    for p in range(2):
        await_corners(0, p)
    match([(p, across, 1) for p in range(2)] + [(p, along, j) for p in range(2) for j in (0, 2)])
    for p in range(2):
        await_corners(1, p)
    match([(p, across, j) for p in range(2) for j in (0, 2)])

    silent = (s == ns_ - 1) & ((lane8 & 16) != 0)
    found = jnp.where(silent, 0.0, dtile[...])
    dtile[...] = found

    def total_copy(k):
        return remote(dtile, dslots.at[s], ds.at[k], dr.at[s], (k, r, c))

    def total_arrival(k):
        return remote(dtile, dslots.at[k], ds.at[k], dr.at[k], (k, r, c))

    for k in range(ns_ - 1, 0, -1):
        @pl.when(k > s)
        def _(k=k):
            total_copy(k).start()
    for g in range(4):
        out_ref[0, g // 2, :, g % 2] = (pltpu.roll(found, N - 16 * g, 1) if g else found)[0:SIDE, 0:SIDE]
    strips[...] = jnp.zeros_like(strips)

    for k in range(ns_ - 1):
        @pl.when(k < s)
        def _(k=k):
            total_arrival(k).wait_recv()
    lower = dslots[0]
    for k in range(1, ns_ - 1):
        lower = lower + dslots[k]
    second = (lane8 & 16) != 0
    below = lower + jnp.where(second, pltpu.roll(lower, 16, 1), pltpu.roll(lower, N - 16, 1))
    below = below + jnp.where(second, pltpu.roll(found, 16, 1), 0.0)
    ftile[...] = held + pltpu.roll(start - below, 4 * SIDE, 1)
    for b, e in near:
        @pl.when(inside(0, b, e))
        def _(b=b, e=e):
            frame_copy(b, e).start()

    for p in (0, 1):
        for side in range(2):
            @pl.when(inside(-p, 0, 2 * side - 1))
            def _(p=p, side=side):
                col_rim(p, side).wait_send()

            for kind in range(2):
                @pl.when(corner_moves(p, kind, 2 * side - 1))
                def _(p=p, kind=kind, side=side):
                    corner(p, kind, side).wait_send()

        for kind in range(2):
            for k in range(LEGS):
                for m in range(PARTS[kind]):
                    @pl.when(leg_goes(p, kind, k, m))
                    def _(p=p, kind=kind, k=k, m=m):
                        for block in range(SIDE) if k == LEGS - 1 else (None,):
                            leg(p, kind, k, m, block).wait_send()

    @pl.when(s > 0)
    def _():
        tile_copy().wait_send()

    for k in range(1, ns_):
        @pl.when(k > s)
        def _(k=k):
            total_copy(k).wait_send()
    for b, e in near:
        @pl.when(inside(0, b, e))
        def _(b=b, e=e):
            frame_copy(b, e).wait_send()
            frame_copy(-b, -e).wait_recv()

    for b in (-1, 0, 1):
        for e in (-1, 0, 1):
            at = SIDE * (b + 1)
            tile = ftile[...] if (b, e) == (0, 0) else fslots[3 * (b + 1) + e + 1]
            strips[e + 1, at : at + SIDE, :] = tile[0:SIDE]
    lane16 = iota((16, N), 1) & 15

    def frame(q):
        out = jnp.zeros((16, N), F32)
        for e in (-1, 0, 1):
            at = SIDE * (e + 1)
            by = (at - SIDE * q) % N
            strip = strips[e + 1]
            strip = pltpu.roll(strip, by, 1) if by else strip
            out = jnp.where((lane16 >= at) & (lane16 < at + SIDE), strip, out)
        return out

    v, right, down, anchor, target = (frame(q) for q in range(5))
    right_left = pltpu.roll(right, 1, 1)
    down_upper = pltpu.roll(down, 1, 0)
    for _ in range(ITERS):
        v = (
            v
            + right * (pltpu.roll(v, N - 1, 1) - v)
            + right_left * (pltpu.roll(v, 1, 1) - v)
            + down * (pltpu.roll(v, 15, 0) - v)
            + down_upper * (pltpu.roll(v, 1, 0) - v)
            + anchor * (target - v)
        )
    v = pltpu.roll(v, 16 - SIDE, 0)
    for g in range(4):
        out_ref[1, g // 2, :, g % 2] = pltpu.roll(v, (N - 16 * g - SIDE) % N, 1)[0:SIDE, 0:SIDE]


def per_device(sizes, images, offsets, warp, stiffness, valid):
    vmem = pl.BlockSpec(memory_space=pltpu.VMEM)
    anywhere = pl.BlockSpec(memory_space=pl.ANY)
    dma = pltpu.SemaphoreType.DMA
    out = jax.ShapeDtypeStruct((2, 2, SIDE, 2, SIDE), F32)
    n = sizes[0]
    turned = (0, 2, 1, 3)
    outs = pl.pallas_call(
        functools.partial(kernel, sizes),
        name="align",
        out_shape=out,
        in_specs=[anywhere] * 6,
        out_specs=vmem,
        scratch_shapes=[
            pltpu.SMEM((2, SIDE, 2, SIDE), jnp.int32),
            pltpu.VMEM((2, SIDE, 2, SIDE), F32),
            pltpu.VMEM((2, SIDE, 2, SIDE), F32),
            pltpu.VMEM((SIDE, 2, SIDE), jnp.int32),
            pltpu.VMEM((2 * N, 6 * N), BF),
            pltpu.VMEM((TILE, TILE), F32),
            pltpu.VMEM((2, TILE + 2 * HALF, TILE + 2 * N), F32),
            pltpu.VMEM((18, N, N), F32),
            pltpu.VMEM((2, 2, TILE // 2, N), F32),
            pltpu.VMEM((2, 2, TILE // 2, N), F32),
            pltpu.VMEM((2, 2, LEGS - 1, HALF, TILE), F32),
            pltpu.VMEM((2, 2, 2, HALF // 2, N), F32),
            pltpu.VMEM((2, 2, 2, HALF // 2, N), F32),
            pltpu.VMEM((10, 8, N), F32),
            pltpu.VMEM((8, N), F32),
            pltpu.VMEM((9, 8, N), F32),
            pltpu.VMEM((8, N), F32),
            pltpu.VMEM((n, 8, N), F32),
            pltpu.VMEM((3, 16, N), F32),
            dma((7,)),
            dma((1,)),
            dma((1,)),
            dma((4 * PARTS[1] * (LEGS + 2),)),
            dma((4 * PARTS[1] * (LEGS + 2),)),
            dma((4,)),
            dma((4,)),
            dma((8,)),
            dma((8,)),
            dma((n,)),
            dma((n,)),
            dma((9,)),
            dma((9,)),
        ],
        compiler_params=pltpu.CompilerParams(
            collective_id=0, has_side_effects=True, vmem_limit_bytes=60 * 1024 * 1024
        ),
    )(
        images,
        offsets.transpose(turned),
        warp.transpose(turned),
        stiffness.transpose(turned),
        valid.transpose(1, 0, 2),
        jnp.asarray(tables()),
    )
    return tuple(x.transpose(turned) for x in outs)


def solution(mesh):
    sizes = tuple(mesh.shape[a] for a in ("sec", "row", "col"))
    return jax.shard_map(
        functools.partial(per_device, sizes),
        mesh=mesh,
        in_specs=(
            P("sec", "row", "col"),
            P(None, "sec", "row", "col"),
            P(None, "sec", "row", "col"),
            P(None, "sec", "row", "col"),
            P("sec", "row", "col"),
        ),
        out_specs=(P(None, "sec", "row", "col"), P(None, "sec", "row", "col")),
        check_vma=False,
    )
```

```python
import functools

import jax
import jax.numpy as jnp
import ml_dtypes
import numpy as np
from jax import lax
from jax.experimental import pallas as pl
from jax.experimental.pallas import tpu as pltpu
from jax.sharding import PartitionSpec as P

MESH = pl.DeviceIdType.MESH
N = 128
HALF = 64
SIDE = 3
TILE = SIDE * N
BLOCKS = 2 * TILE // N
SHARPNESS = 80.0
ANCHOR = 0.2
ITERS = 3
LEGS = 4
PARTS = (4, 4)
BF = jnp.bfloat16
F32 = jnp.float32


def split3(a):
    high = a.astype(ml_dtypes.bfloat16)
    rest = a - high.astype(np.float64)
    mid = rest.astype(ml_dtypes.bfloat16)
    low = (rest - mid.astype(np.float64)).astype(ml_dtypes.bfloat16)
    return high, mid, low


def tables():
    x = np.arange(N)
    forward = np.zeros((N, N))
    for f in range(HALF):
        forward[f] = np.cos(2 * np.pi * ((f * x) % N) / N)
    forward[HALF] = 1 - 2 * (x % 2)
    for f in range(1, HALF):
        forward[HALF + f] = np.sin(2 * np.pi * ((f * x) % N) / N)
    scale = np.full(N, 2.0 / N)
    scale[0] = scale[HALF] = 1.0 / N
    inverse = (forward * scale[:, None]).T

    def right(a):
        h, m, l = split3(a)
        return np.block([[h, m], [h, m]]), np.concatenate([h, l], 0)

    return np.concatenate([*right(forward.T), *right(inverse.T * np.sqrt(SHARPNESS / (N * N)))], 1)


def parts(x):
    high = x.astype(BF)
    rest = x - high.astype(F32)
    mid = rest.astype(BF)
    low = (rest - mid.astype(F32)).astype(BF)
    return high, mid, low


def dot(a, b):
    return jnp.dot(a, b, preferred_element_type=F32)


def right_mul(x, wa, wb):
    high, mid, low = parts(x)
    a = dot(jnp.concatenate([high, mid], 1), wa)
    return a[:, :N] + a[:, N:] + dot(jnp.concatenate([low, high], 1), wb)


def turn(x):
    return jnp.concatenate([x[k : k + N].T for k in range(0, x.shape[0], N)], 0)


def forward(x, t):
    return right_mul(turn(right_mul(x, t[:, 0 : 2 * N], t[:, 2 * N : 3 * N])), t[:, 0 : 2 * N], t[:, 2 * N : 3 * N])


def inverse(x, t):
    return right_mul(turn(right_mul(x, t[:, 3 * N : 5 * N], t[:, 5 * N :])), t[:, 3 * N : 5 * N], t[:, 5 * N :])


def iota(shape, dim):
    return lax.broadcasted_iota(jnp.int32, shape, dim)


def swap(x):
    return pltpu.roll(x, HALF, 1)


def cross(mine, theirs):
    lane = iota((N, N), 1)
    single = (lane & (HALF - 1)) == 0
    turned = swap(theirs)
    first = jnp.where(single | (lane < HALF), theirs, -turned)
    second = jnp.where(single, 0.0, jnp.where(lane < HALF, turned, theirs))
    other = swap(mine)
    even, odd = slice(0, HALF), slice(HALF, N)

    def pair(a, b):
        return mine[a] * first[b] + other[a] * second[b]

    lone = iota((HALF, N), 0) == 0
    both = pair(odd, odd)
    top = pair(even, even) + jnp.where(lone, 0.0, both)
    top = jnp.where(lone & (iota((HALF, N), 1) == 0), 0.0, top)
    low = jnp.where(lone, both, pair(even, odd) - pair(odd, even))
    return jnp.concatenate([top, low], 0)


def peaks(scores, shifts):
    count = len(shifts)
    blocks = [scores[k * N : k * N + N] for k in range(count)]
    highest = jnp.concatenate([jnp.max(x, axis=0, keepdims=True) for x in blocks], 0)
    highest = jnp.max(highest, axis=1, keepdims=True)
    sums = []
    for k, (dy, dx) in enumerate(shifts):
        rows = (((iota((N, N), 0) - dy + HALF) & (N - 1)) - HALF).astype(F32)
        cols = (((iota((1, N), 1) - dx + HALF) & (N - 1)) - HALF).astype(F32)
        weights = jnp.exp(blocks[k] - highest[k : k + 1])
        by_col = jnp.sum(weights, axis=0, keepdims=True)
        sums.append((by_col, jnp.sum(weights * rows, axis=0, keepdims=True), by_col * cols))
    sums = [jnp.sum(jnp.concatenate([x[q] for x in sums], 0), axis=1, keepdims=True) for q in range(3)]
    return sums[1] / sums[0], sums[2] / sums[0]


class Remote:
    def __init__(self, src, dst, send, recv, target, here):
        self.refs, self.target, self.here = (src, dst, send, recv), target, here

    def to(self, device):
        return pltpu.make_async_remote_copy(*self.refs, device_id=device, device_id_type=MESH)

    def start(self):
        self.to(self.target).start()

    def wait_recv(self):
        self.to(self.here).wait_recv()

    def wait_send(self):
        self.to(self.here).wait_send()


def kernel(sizes, images, off_in, warp_in, stiff_in, valid_in, table, out_ref, *rest):
    (off, warp, stiff, valid, t, own, ext, spec, packed, landed, transit, cpacked, clanded) = rest[:13]
    (small, ftile, fslots, dtile, dslots, strips) = rest[13:19]
    lsem, ts, tr, rs, rr, cs, cr, ks, kr, ds, dr, fs, fr = rest[19:]
    ns_, nr_, nc_ = sizes
    ny_, nz_ = nr_ // 2, 2 * nc_
    hop = nc_ // LEGS
    s, r, c = lax.axis_index("sec"), lax.axis_index("row"), lax.axis_index("col")
    y, half = r // 2, lax.rem(r, 2)
    z = half * nc_ + c

    def inside(a, b, e):
        ok = None
        for at, by, n in ((s, a, ns_), (r, b, nr_), (c, e, nc_)):
            if by:
                here = (at + by >= 0) & (at + by < n)
                ok = here if ok is None else ok & here
        return ok

    def there(a, b, e):
        return (s + a, r + b, c + e)

    def on_line(a, to_y, to_z):
        to_z = lax.rem(to_z + 2 * nz_, nz_)
        return (s + a, 2 * to_y + to_z // nc_, lax.rem(to_z, nc_))

    def half_at(at_z):
        return lax.rem(at_z + 2 * nz_, nz_) // nc_

    barrier = pltpu.get_barrier_semaphore()
    goes = [(k, 0, 0) for k in range(1, ns_)] + [(-1, 0, 0), (-1, 0, -1), (-1, 0, 1), (0, 0, -1), (0, 0, 1)]
    expected = 0
    for a, e in ((0, hop), (0, -hop), (-1, -hop)):
        for b in (-1, 0, 1):
            def both(sign, a=a, b=b):
                return (s + sign * a >= 0) & (s + sign * a < ns_) & (y + sign * b >= 0) & (y + sign * b < ny_)

            @pl.when(both(-1))
            def _(a=a, b=b, e=e):
                pl.semaphore_signal(barrier, inc=1, device_id=on_line(-a, y - b, z - e), device_id_type=MESH)

            expected = expected + both(1).astype(jnp.int32)
    for a, b, e in goes:
        @pl.when(inside(-a, -b, -e))
        def _(a=a, b=b, e=e):
            pl.semaphore_signal(barrier, inc=1, device_id=there(-a, -b, -e), device_id_type=MESH)

        expected = expected + inside(a, b, e).astype(jnp.int32)

    locals_ = [
        pltpu.make_async_copy(src, dst, lsem.at[k])
        for k, (src, dst) in enumerate(
            (
                (images.at[1], ext.at[0, HALF : HALF + TILE, N : N + TILE]),
                (images.at[0], own),
                (table, t),
                (off_in, off),
                (warp_in, warp),
                (stiff_in, stiff),
                (valid_in, valid),
            )
        )
    ]
    for copy in locals_:
        copy.start()

    @pl.when(r == 0)
    def _():
        for p in range(2):
            ext[p, 0:HALF, :] = jnp.zeros((HALF, TILE + 2 * N), F32)

    @pl.when(r == nr_ - 1)
    def _():
        for p in range(2):
            ext[p, HALF + TILE :, :] = jnp.zeros((HALF, TILE + 2 * N), F32)

    @pl.when(c == 0)
    def _():
        for p in range(2):
            ext[p, 0:HALF, 0:N] = jnp.zeros((HALF, N), F32)
            ext[p, HALF + TILE :, 0:N] = jnp.zeros((HALF, N), F32)
            landed[p, 0] = jnp.zeros((TILE // 2, N), F32)

    @pl.when(c == nc_ - 1)
    def _():
        for p in range(2):
            ext[p, 0:HALF, N + TILE :] = jnp.zeros((HALF, N), F32)
            ext[p, HALF + TILE :, N + TILE :] = jnp.zeros((HALF, N), F32)
            landed[p, 1] = jnp.zeros((TILE // 2, N), F32)

    @pl.when(s == ns_ - 1)
    def _():
        ext[1] = jnp.zeros((TILE + 2 * HALF, TILE + 2 * N), F32)
        landed[1] = jnp.zeros((2, TILE // 2, N), F32)

    near = [(b, e) for b in (1, -1, 0) for e in (0, -1, 1) if (b, e) != (0, 0)]
    blank = jnp.zeros((8, N), F32)
    for b, e in near:
        @pl.when(jnp.logical_not(inside(0, b, e)))
        def _(b=b, e=e):
            fslots[3 * (b + 1) + e + 1] = blank

    for k in range(ns_):
        @pl.when(s <= k)
        def _(k=k):
            dslots[k] = blank

    def pack(strip, side):
        count = strip.shape[0] // 2
        upper, lower = strip[:count], strip[count:]
        low = iota((count, N), 1) < HALF
        return jnp.where(low, swap(upper), lower) if side else jnp.where(low, upper, swap(lower))

    def unpack(got, side):
        turned = swap(got)
        return (got, turned) if side else (turned, got)

    def mine_spectra(p):
        def step(i, _):
            at = pl.multiple_of(i * N, N)
            if p == 0:
                blocks = [own[pl.ds(at, N), j * N : j * N + N] for j in range(SIDE)]
            else:
                at = pl.multiple_of(at + HALF, HALF)
                blocks = [ext[0, pl.ds(at, N), j * N + N : j * N + 2 * N] for j in range(SIDE)]
            found = forward(jnp.concatenate(blocks, 0), t)
            for j in range(SIDE):
                spec[9 * p + SIDE * i + j] = found[j * N : j * N + N]
            return 0

        lax.fori_loop(0, SIDE, step, 0)

    pl.semaphore_wait(barrier, expected)

    def remote(src, dst, send, recv, target):
        return Remote(src, dst, send, recv, target, (s, r, c))

    def col_rim(p, side):
        e = 2 * side - 1
        return remote(
            packed.at[1 - p, side], landed.at[p, 1 - side], cs.at[2 * p + side], cr.at[2 * p + 1 - side], there(-p, 0, e)
        )

    def tile_copy():
        return remote(images.at[0], ext.at[1, HALF : HALF + TILE, N : N + TILE], ts.at[0], tr.at[0], there(-1, 0, 0))

    turn_y = 2 * half - 1
    has_cross = (y + turn_y >= 0) & (y + turn_y < ny_)
    first_at, last_at = 0, HALF + TILE

    def takes(at_y):
        return ny_ - 1 - at_y

    def rows_of(kind):
        return HALF // PARTS[kind]

    def rim_at(kind, of_half):
        return of_half * last_at if kind else (1 - of_half) * last_at

    def leg(p, kind, k, m, block=None):
        sign = 1 - 2 * p
        n = rows_of(kind)
        index = (p * 2 + kind) * PARTS[1] + m
        index = index * (LEGS - 1) + k if block is None else 4 * PARTS[1] * (LEGS - 1) + index * SIDE + block
        lanes = slice(0, TILE) if block is None else slice(block * N, block * N + N)
        if k == 0:
            top = pl.multiple_of((half if kind else 1 - half) * (TILE - HALF) + m * n, 8)
            src = images.at[1 - p, pl.ds(top, n), :]
            to_y = y
            if kind:
                early = ((half == 1) & (m >= takes(y))) | ((half == 0) & (m < takes(y - 1)))
                to_y = jnp.where(early, y + turn_y, y)
            target = on_line(-p, to_y, z + sign * hop)
        else:
            src = transit.at[p, kind, k - 1, pl.ds(m * n, n), lanes]
            to_y = y
            if kind and k == LEGS - 1:
                from_half = half_at(z - sign * hop * k)
                late = ((from_half == 1) & (m < takes(y))) | ((from_half == 0) & (m > takes(y)))
                to_y = jnp.where(late, y + 2 * from_half - 1, y)
            target = on_line(0, to_y, z + sign * hop)
        if k == LEGS - 1:
            at = pl.multiple_of(rim_at(kind, half_at(z + sign * hop)) + m * n, 8)
            dst = ext.at[p, pl.ds(at, n), lanes.start + N : lanes.stop + N]
        else:
            dst = transit.at[p, kind, k, pl.ds(m * n, n), :]
        return remote(src, dst, rs.at[index], rr.at[index], target)

    def leg_comes(p, kind, k, m):
        ok = s + p < ns_
        if kind:
            ok = ok & (has_cross if k == LEGS - 1 else m != takes(y))
        return ok

    def leg_goes(p, kind, k, m):
        if k:
            return leg_comes(p, kind, k - 1, m)
        return (s - p >= 0) & has_cross if kind else s - p >= 0

    def begin(kind, pairs=(0, 1)):
        for m in range(PARTS[kind]):
            for p in pairs:
                @pl.when(leg_goes(p, kind, 0, m))
                def _(p=p, m=m):
                    leg(p, kind, 0, m).start()

    def each_part(kind, condition, k, act):
        for m in range(PARTS[kind]):
            for p in range(2):
                @pl.when(condition(p, kind, k, m))
                def _(p=p, m=m):
                    act(p, m)

    def pass_on(kind, k):
        def act(p, m):
            leg(p, kind, k, m).wait_recv()
            if k < LEGS - 2:
                leg(p, kind, k + 1, m).start()
            else:
                leg(p, kind, k + 1, m, 0).start()
                leg(p, kind, k + 1, m, SIDE - 1).start()

        each_part(kind, leg_comes, k, act)
        if k == LEGS - 2:
            each_part(kind, leg_comes, k, lambda p, m: leg(p, kind, k + 1, m, 1).start())

    def arrive(kind, blocks):
        def act(p, m):
            for block in blocks:
                leg(p, kind, LEGS - 1, m, block).wait_recv()

        each_part(kind, leg_comes, LEGS - 1, act)

    def corner(p, kind, side):
        n = 4 * p + 2 * kind
        return remote(
            cpacked.at[p, kind, side],
            clanded.at[p, kind, 1 - side],
            ks.at[n + side],
            kr.at[n + 1 - side],
            there(0, 0, 2 * side - 1),
        )

    def rim_rows(kind):
        return pl.ds(pl.multiple_of(rim_at(kind, half), HALF), HALF)

    def corner_moves(p, kind, e):
        ok = (s + p < ns_) & inside(0, 0, e)
        return ok & has_cross if kind else ok

    def send_corners(kind):
        for p in range(2):
            for side in range(2):
                @pl.when(corner_moves(p, kind, 2 * side - 1))
                def _(p=p, side=side):
                    src = slice(TILE, TILE + N) if side else slice(N, 2 * N)
                    cpacked[p, kind, side] = pack(ext[p, rim_rows(kind), src], side)
                    corner(p, kind, side).start()

    def await_corners(kind, p):
        for side in range(2):
            @pl.when(corner_moves(p, kind, 1 - 2 * side))
            def _(side=side):
                corner(p, kind, side).wait_recv()
                dst = slice(0, N) if side else slice(N + TILE, 2 * N + TILE)
                ext[p, rim_rows(kind), dst] = jnp.concatenate(unpack(clanded[p, kind, 1 - side], 1 - side), 0)

    def frame_copy(b, e):
        n, m = 3 * (b + 1) + e + 1, 3 * (1 - b) + 1 - e
        return remote(ftile.at[0:4], fslots.at[m, 0:4], fs.at[n], fr.at[m], there(0, b, e))

    def match(vertices):
        lane = iota((N, N), 1)
        row = iota((N, N), 0)
        low = lane < HALF
        found = dtile[...]
        stack = []
        for p, i, j in vertices:
            top = i * N

            def at(first, rows, block):
                if not isinstance(i, int):
                    first = pl.multiple_of(first, HALF)
                return ext[p, pl.ds(first, rows), block * N : block * N + N]

            def beside(first, rows):
                left, right = at(first, rows, j), at(first, rows, j + 2)
                return jnp.where(low[:rows], right, left)

            dy, dx = off[0, i, p, j], off[1, i, p, j]
            in_rows = (row >= dy) & (row < dy + N)
            in_cols = (lane >= dx) & (lane < dx + N)
            main = jnp.where(in_cols, at(top + HALF, N, j + 1), beside(top + HALF, N))
            over = jnp.concatenate([at(top + HALF + N, HALF, j + 1), at(top, HALF, j + 1)], 0)
            over_side = jnp.concatenate([beside(top + HALF + N, HALF), beside(top, HALF)], 0)
            stack.append(jnp.where(in_rows, main, jnp.where(in_cols, over, over_side)))
        theirs = forward(jnp.concatenate(stack, 0), t)
        scores = inverse(
            jnp.concatenate(
                [cross(spec[9 * p + SIDE * i + j], theirs[k * N : k * N + N]) for k, (p, i, j) in enumerate(vertices)], 0
            ),
            t,
        )
        shifts = [(off[0, i, p, j], off[1, i, p, j]) for p, i, j in vertices]
        for comp, found_shifts in enumerate(peaks(scores, shifts)):
            for k, (p, i, j) in enumerate(vertices):
                value = (shifts[k][comp].astype(F32) + found_shifts[k : k + 1]) * (1.0 / N)
                found = jnp.where((row8 == i) & (lane8 == 16 * (2 * comp + p) + j), value, found)
        dtile[...] = found

    def match_row(p, i):
        match([(p, i, j) for j in range(SIDE)])

    def fill_columns(p):
        for side in range(2):
            @pl.when(inside(p, 0, 1 - 2 * side))
            def _(side=side):
                col_rim(p, side).wait_recv()
        for side in range(2):
            column = slice(0, N) if side == 0 else slice(N + TILE, 2 * N + TILE)
            upper, lower = unpack(landed[p, side], side)
            ext[p, HALF : HALF + TILE // 2, column] = upper
            ext[p, HALF + TILE // 2 : HALF + TILE, column] = lower

    begin(0)
    begin(1)

    @pl.when(s > 0)
    def _():
        tile_copy().start()

    for copy in locals_[:2]:
        copy.wait()
    for im in range(2):
        for side in range(2):
            if im == 0:
                strip = own[:, 0:N] if side == 0 else own[:, TILE - N :]
            else:
                strip = ext[0, HALF : HALF + TILE, N : 2 * N] if side == 0 else ext[0, HALF : HALF + TILE, TILE : TILE + N]
            packed[im, side] = pack(strip, side)
    for p in (0, 1):
        for side in range(2):
            @pl.when(inside(-p, 0, 2 * side - 1))
            def _(p=p, side=side):
                col_rim(p, side).start()

    for copy in locals_[2:]:
        copy.wait()
    mine_spectra(0)
    pass_on(0, 0)
    pass_on(1, 0)
    row8, lane8 = iota((8, N), 0), iota((8, N), 1)
    small[...] = jnp.zeros_like(small)
    for comp in range(2):
        for sec in range(2):
            small[2 * comp + sec, 0:SIDE, 0:SIDE] = warp[comp, :, sec]
            small[4 + 2 * comp + sec, 0:SIDE, 0:SIDE] = stiff[comp, :, sec]
    for sec in range(2):
        small[8 + sec, 0:SIDE, 0:SIDE] = ANCHOR * valid[:, sec].astype(F32)
    dtile[...] = blank
    start = jnp.zeros((8, N), F32)
    held = jnp.zeros((8, N), F32)
    for g in range(4):
        sec = g % 2
        w = small[g]
        right = jnp.where((c == nc_ - 1) & (lane8 == SIDE - 1), 0.0, small[4 + sec])
        down = jnp.where((r == nr_ - 1) & (row8 == SIDE - 1), 0.0, small[6 + sec])
        start = start + (pltpu.roll(w, 16 * g, 1) if g else w)
        for q, quantity in enumerate((w, right, down, small[8 + sec])):
            by = 16 * g + SIDE * q
            held = held + (pltpu.roll(quantity, by, 1) if by else quantity)

    mine_spectra(1)
    fill_columns(0)
    for k in range(1, LEGS - 1):
        pass_on(0, k)
        pass_on(1, k)
        if k == 1:
            match_row(0, 1)
    if LEGS < 3:
        match_row(0, 1)

    @pl.when(s < ns_ - 1)
    def _():
        tile_copy().wait_recv()

    fill_columns(1)
    match_row(1, 1)
    along, across = 2 * (1 - half), 2 * half
    arrive(0, (0, SIDE - 1))
    send_corners(0)
    arrive(0, (1,))
    match([(p, along, 1) for p in range(2)])
    arrive(1, (0, SIDE - 1))
    send_corners(1)
    arrive(1, (1,))
    for p in range(2):
        await_corners(0, p)
    match([(p, across, 1) for p in range(2)] + [(p, along, j) for p in range(2) for j in (0, 2)])
    for p in range(2):
        await_corners(1, p)
    match([(p, across, j) for p in range(2) for j in (0, 2)])

    silent = (s == ns_ - 1) & ((lane8 & 16) != 0)
    found = jnp.where(silent, 0.0, dtile[...])
    dtile[...] = found

    def total_copy(k):
        return remote(dtile, dslots.at[s], ds.at[k], dr.at[s], (k, r, c))

    def total_arrival(k):
        return remote(dtile, dslots.at[k], ds.at[k], dr.at[k], (k, r, c))

    for k in range(ns_ - 1, 0, -1):
        @pl.when(k > s)
        def _(k=k):
            total_copy(k).start()
    for g in range(4):
        out_ref[0, g // 2, :, g % 2] = (pltpu.roll(found, N - 16 * g, 1) if g else found)[0:SIDE, 0:SIDE]
    strips[...] = jnp.zeros_like(strips)

    for k in range(ns_ - 1):
        @pl.when(k < s)
        def _(k=k):
            total_arrival(k).wait_recv()
    lower = dslots[0]
    for k in range(1, ns_ - 1):
        lower = lower + dslots[k]
    second = (lane8 & 16) != 0
    below = lower + jnp.where(second, pltpu.roll(lower, 16, 1), pltpu.roll(lower, N - 16, 1))
    below = below + jnp.where(second, pltpu.roll(found, 16, 1), 0.0)
    ftile[...] = held + pltpu.roll(start - below, 4 * SIDE, 1)
    for b, e in near:
        @pl.when(inside(0, b, e))
        def _(b=b, e=e):
            frame_copy(b, e).start()

    for p in (0, 1):
        for side in range(2):
            @pl.when(inside(-p, 0, 2 * side - 1))
            def _(p=p, side=side):
                col_rim(p, side).wait_send()

            for kind in range(2):
                @pl.when(corner_moves(p, kind, 2 * side - 1))
                def _(p=p, kind=kind, side=side):
                    corner(p, kind, side).wait_send()

        for kind in range(2):
            for k in range(LEGS):
                for m in range(PARTS[kind]):
                    @pl.when(leg_goes(p, kind, k, m))
                    def _(p=p, kind=kind, k=k, m=m):
                        for block in range(SIDE) if k == LEGS - 1 else (None,):
                            leg(p, kind, k, m, block).wait_send()

    @pl.when(s > 0)
    def _():
        tile_copy().wait_send()

    for k in range(1, ns_):
        @pl.when(k > s)
        def _(k=k):
            total_copy(k).wait_send()
    for b, e in near:
        @pl.when(inside(0, b, e))
        def _(b=b, e=e):
            frame_copy(b, e).wait_send()
            frame_copy(-b, -e).wait_recv()

    for b in (-1, 0, 1):
        for e in (-1, 0, 1):
            at = SIDE * (b + 1)
            tile = ftile[...] if (b, e) == (0, 0) else fslots[3 * (b + 1) + e + 1]
            strips[e + 1, at : at + SIDE, :] = tile[0:SIDE]
    lane16 = iota((16, N), 1) & 15

    def frame(q):
        out = jnp.zeros((16, N), F32)
        for e in (-1, 0, 1):
            at = SIDE * (e + 1)
            by = (at - SIDE * q) % N
            strip = strips[e + 1]
            strip = pltpu.roll(strip, by, 1) if by else strip
            out = jnp.where((lane16 >= at) & (lane16 < at + SIDE), strip, out)
        return out

    v, right, down, anchor, target = (frame(q) for q in range(5))
    right_left = pltpu.roll(right, 1, 1)
    down_upper = pltpu.roll(down, 1, 0)
    for _ in range(ITERS):
        v = (
            v
            + right * (pltpu.roll(v, N - 1, 1) - v)
            + right_left * (pltpu.roll(v, 1, 1) - v)
            + down * (pltpu.roll(v, 15, 0) - v)
            + down_upper * (pltpu.roll(v, 1, 0) - v)
            + anchor * (target - v)
        )
    v = pltpu.roll(v, 16 - SIDE, 0)
    for g in range(4):
        out_ref[1, g // 2, :, g % 2] = pltpu.roll(v, (N - 16 * g - SIDE) % N, 1)[0:SIDE, 0:SIDE]


def per_device(sizes, images, offsets, warp, stiffness, valid):
    vmem = pl.BlockSpec(memory_space=pltpu.VMEM)
    anywhere = pl.BlockSpec(memory_space=pl.ANY)
    dma = pltpu.SemaphoreType.DMA
    out = jax.ShapeDtypeStruct((2, 2, SIDE, 2, SIDE), F32)
    n = sizes[0]
    turned = (0, 2, 1, 3)
    outs = pl.pallas_call(
        functools.partial(kernel, sizes),
        name="align",
        out_shape=out,
        in_specs=[anywhere] * 6,
        out_specs=vmem,
        scratch_shapes=[
            pltpu.SMEM((2, SIDE, 2, SIDE), jnp.int32),
            pltpu.VMEM((2, SIDE, 2, SIDE), F32),
            pltpu.VMEM((2, SIDE, 2, SIDE), F32),
            pltpu.VMEM((SIDE, 2, SIDE), jnp.int32),
            pltpu.VMEM((2 * N, 6 * N), BF),
            pltpu.VMEM((TILE, TILE), F32),
            pltpu.VMEM((2, TILE + 2 * HALF, TILE + 2 * N), F32),
            pltpu.VMEM((18, N, N), F32),
            pltpu.VMEM((2, 2, TILE // 2, N), F32),
            pltpu.VMEM((2, 2, TILE // 2, N), F32),
            pltpu.VMEM((2, 2, LEGS - 1, HALF, TILE), F32),
            pltpu.VMEM((2, 2, 2, HALF // 2, N), F32),
            pltpu.VMEM((2, 2, 2, HALF // 2, N), F32),
            pltpu.VMEM((10, 8, N), F32),
            pltpu.VMEM((8, N), F32),
            pltpu.VMEM((9, 8, N), F32),
            pltpu.VMEM((8, N), F32),
            pltpu.VMEM((n, 8, N), F32),
            pltpu.VMEM((3, 16, N), F32),
            dma((7,)),
            dma((1,)),
            dma((1,)),
            dma((4 * PARTS[1] * (LEGS + 2),)),
            dma((4 * PARTS[1] * (LEGS + 2),)),
            dma((4,)),
            dma((4,)),
            dma((8,)),
            dma((8,)),
            dma((n,)),
            dma((n,)),
            dma((9,)),
            dma((9,)),
        ],
        compiler_params=pltpu.CompilerParams(
            collective_id=0, has_side_effects=True, vmem_limit_bytes=60 * 1024 * 1024
        ),
    )(
        images,
        offsets.transpose(turned),
        warp.transpose(turned),
        stiffness.transpose(turned),
        valid.transpose(1, 0, 2),
        jnp.asarray(tables()),
    )
    return tuple(x.transpose(turned) for x in outs)


def solution(mesh):
    sizes = tuple(mesh.shape[a] for a in ("sec", "row", "col"))
    return jax.shard_map(
        functools.partial(per_device, sizes),
        mesh=mesh,
        in_specs=(
            P("sec", "row", "col"),
            P(None, "sec", "row", "col"),
            P(None, "sec", "row", "col"),
            P(None, "sec", "row", "col"),
            P("sec", "row", "col"),
        ),
        out_specs=(P(None, "sec", "row", "col"), P(None, "sec", "row", "col")),
        check_vma=False,
    )
```
